256 devices in a mesh: inst: 32 (over x, z_hi, core), head: 8 (over z_lo, y).
Axes of the slice: x: 4, y: 4, z: 8 (z_hi: 4, z_lo: 2; z = z_hi * 2 + z_lo), core: 2. Of those that a mesh axis runs over, the one named last changes fastest.
Arguments:
- latent_cache: bfloat16 [256, 1024, 576], P('inst', 'head'), may hold values from -6 to 6
- cache_lengths: int32 [256], P('inst'), may hold values from 1 to 1024, as said below
- partner: int32 [32], replicated, may hold values from 0 to 31, as said below
- queries: bfloat16 [4, 256, 128, 576], P(None, 'inst', 'head'), may hold values from -240 to 240
- step_rows: bfloat16 [4, 256, 576], P(None, 'inst'), may hold values from -6 to 6
- arrivals: bfloat16 [65536, 576], P(('inst', 'head')), may hold values from -6 to 6
- arrival_routes: int32 [65536, 1], P(('inst', 'head')), may hold values from 0 to 31; in each aligned block of 256 rows (0 to 255, 256 to 511, ...) at most 16 rows name the same one
- arrival_owners: int32 [65536], P(('inst', 'head')), may hold values from 0 to 3
- new_queries: bfloat16 [4, 128, 128, 576], P(None, 'inst', 'head'), may hold values from -240 to 240
- new_step_rows: bfloat16 [4, 128, 576], P(None, 'inst'), may hold values from -6 to 6
- value_up: bfloat16 [128, 512, 128], P('head'), may hold values from -0.25 to 0.25
Outputs:
- resident_out: bfloat16 [4, 256, 16384], P(None, 'inst', 'head')
- arrival_out: bfloat16 [4, 128, 16384], P(None, 'inst', 'head')
The draws below stay inside these ranges and needn't reach their ends.
Inputs may be any that keep to these rules, and one draw needn't show every extreme that they name: `cache_lengths`: every resident request has 1 to 1024 valid positions; some has exactly 1024, some exactly 1. partner is a perfect matching: partner[partner[i]] = i and partner[i] != i. `arrival_routes`: among the rows of one device, no instance is named by more than 16 rows.
All inputs are finite; a program needn't handle non-finite values.
Results may differ from the reference program's by a relative error of at most 0.012.
Values may be sent and summed in bfloat16 or wider, within the bound.
No kernel may reach another device: no remote copies, remote signals or barrier semaphores. Data moves between devices by JAX's collectives and lax.ppermute only.
A program may use at most 128 MiB of HBM per device.

```python
import math
import jax
import jax.numpy as jnp
import numpy as np
from jax import lax

H = 128
LATENT_WIDTH = 512
KR = 64
VD = 128
STEPS = 4
RES_DEV = 8
CTX = 1024
MIG = 1
NEW_DEV = 4
PACK_DEV = 256
KD = 576
CAP_DEV = 16
SLOTS = 4096
REQS = 256
NEWS = 128
ROWS = 65536
N_INST = 32


def normal_queries(key, count):
    values = jnp.clip(jax.random.normal(key, (STEPS, count, H, KD), jnp.float32), -6.0, 6.0)
    return values


def draw_cache_lengths(key, part):
    key = jax.random.fold_in(key, 1)
    values = jax.random.randint(key, (REQS,), 1, CTX + 1)
    values = values.at[0].set(CTX).at[1].set(1)
    return values.astype(jnp.int32)


def draw_partner(key, part):
    key = jax.random.fold_in(key, 2)
    order = jax.random.permutation(key, N_INST)
    firsts = order[0::2]
    seconds = order[1::2]
    matched = jnp.zeros((N_INST,), jnp.int32).at[firsts].set(seconds).at[seconds].set(firsts)
    return matched.astype(jnp.int32)


def draw_queries(key, part):
    key = jax.random.fold_in(key, 3)
    return normal_queries(key, REQS).astype(jnp.bfloat16)


def draw_new_queries(key, part):
    key = jax.random.fold_in(key, 4)
    return normal_queries(key, NEWS).astype(jnp.bfloat16)


def place_ends(result, key, low, high):
    shape = result.shape
    index_at = [jax.random.randint(jax.random.fold_in(key, axis), (), 0, shape[axis]) for axis in range(len(shape))]
    result = result.at[tuple(index_at)].set(low)
    longest = shape.index(max(shape))
    index_at[longest] = (index_at[longest] + 1) % shape[longest]
    return result.at[tuple(index_at)].set(high)


def levels(stream_key, shape, cuts, smallest, largest):
    def one(dim, shards_of):
        heights = jax.random.uniform(jax.random.fold_in(jax.random.fold_in(stream_key, 6), dim), (shards_of,), jnp.float32, smallest / len(cuts), largest / len(cuts))
        return jnp.repeat(jnp.exp(heights), shape[dim] // shards_of).reshape((-1,) + (1,) * (len(shape) - dim - 1))

    level = one(*cuts[0])
    for cut in cuts[1:]:
        level = level * one(*cut)
    return level


def routed_block(own_key, own, number, rows, number_of, top, bound, slope):
    ranking = jax.random.permutation(own_key, number_of)
    packed, usual = load_shares(number_of, rows * top, bound, slope, True), load_shares(number_of, rows * top, bound, slope, False)
    places = jnp.arange(number_of)

    def named(sizes, rotation):
        used = int((sizes > 0).sum())
        fixed = max(1, used // 4)
        shifted = fixed + (places - fixed + rotation * (used - fixed)) % max(1, number_of - fixed)
        return jnp.zeros((number_of,), jnp.int32).at[ranking[jnp.where(places < fixed, places, shifted)]].set(jnp.asarray(sizes, jnp.int32))

    sizes = jnp.where(number % 4 == 0, named(packed, number // 4), named(usual, number - number // 4 - 1))
    mixed = jax.random.permutation(jax.random.fold_in(own, 3), number_of)
    giver, taker = mixed[0:number_of // 2 * 2:2], mixed[1:number_of // 2 * 2:2]
    room = jnp.minimum(sizes[giver] - 1, bound - sizes[taker]) // 2
    room = jnp.where((giver == ranking[0]) | (taker == ranking[0]) | (sizes[taker] == 0), 0, jnp.maximum(room, 0))
    shifted = jax.random.randint(jax.random.fold_in(own, 4), (number_of // 2,), 0, 1 << 20) % (room + 1)
    sizes = sizes.at[giver].add(-shifted).at[taker].add(shifted)
    members = jnp.searchsorted(jnp.cumsum(sizes), jnp.arange(rows * top), side="right").astype(jnp.int32)
    table = members.reshape(top, rows).T
    table = table[jax.random.permutation(jax.random.fold_in(own, 1), rows)]
    rotation = jax.random.randint(jax.random.fold_in(own, 2), (rows, 1), 0, top)
    return jnp.take_along_axis(table, (jnp.arange(top)[None, :] + rotation) % top, axis=1)


def load_shares(number_of, total, bound, skew, full):
    weights = [(1 << 20) // math.isqrt(grade ** skew) + 1 for grade in range(1, number_of + 1)]
    largest = bound if full else min(bound, max(-(-total // number_of), total * weights[0] // sum(weights)))
    least = 1 if total - largest >= number_of - 1 else 0
    given, spare = [largest] + [least] * (number_of - 1), total - largest - least * (number_of - 1)
    while spare > 0:
        movable = [i for i in range(1, number_of) if given[i] < largest] or [i for i in range(1, number_of) if given[i] < bound]
        pool, budget = sum([weights[i] for i in movable]), spare
        for i in movable:
            addition = min(bound - given[i], max(1, budget * weights[i] // pool), spare)
            given[i] = given[i] + addition
            spare = spare - addition
    return np.array(given)


def normal_values(own_key, dims, width, reach, pieces=(), kind=jnp.bfloat16):
    array = jax.random.normal(own_key, dims, jnp.float32) * width
    if len(pieces) > 0:
        array = levels(own_key, dims, pieces, -0.22, 0.18) * array
    return jnp.clip(array, min=-reach, max=reach).astype(kind)


def setup_inputs(seed: int = 0) -> dict:
    arg_keys = jax.random.split(jax.random.key(seed), 12)
    latent_cache = normal_values(arg_keys[0], (REQS, CTX, KD), 1.0, 6.0, ((0, 32), (1, 8)))
    cache_lengths = draw_cache_lengths(jax.random.fold_in(arg_keys[11], 71), 0)
    partner = draw_partner(jax.random.fold_in(arg_keys[11], 71), 0)
    queries = draw_queries(jax.random.fold_in(arg_keys[11], 71), 0)
    step_rows = normal_values(arg_keys[4], (STEPS, REQS, KD), 1.0, 6.0, ((1, 32),))
    arrivals = normal_values(arg_keys[5], (ROWS, KD), 1.0, 6.0, ((0, 256),))
    arrival_routes_keys = jax.random.split(jax.random.fold_in(arg_keys[6], 1), ROWS // PACK_DEV)
    arrival_routes_turns = jax.random.permutation(jax.random.fold_in(arg_keys[6], 3), ROWS // PACK_DEV)
    arrival_routes = jax.vmap(lambda own, number: routed_block(jax.random.fold_in(arg_keys[6], 2), own, number, PACK_DEV, N_INST, 1, CAP_DEV, 2))(arrival_routes_keys, arrival_routes_turns).reshape((ROWS, 1))
    arrival_owners = place_ends(jax.random.randint(arg_keys[7], (ROWS,), 0, NEW_DEV), jax.random.fold_in(arg_keys[7], 1), 0, NEW_DEV - 1).astype(jnp.int32)
    new_queries = draw_new_queries(jax.random.fold_in(arg_keys[11], 71), 0)
    new_step_rows = normal_values(arg_keys[9], (STEPS, NEWS, KD), 1.0, 6.0, ((1, 32),))
    value_up = normal_values(arg_keys[10], (H, LATENT_WIDTH, VD), LATENT_WIDTH ** -0.5, 0.25, ((0, 8),))
    return dict(latent_cache=latent_cache, cache_lengths=cache_lengths, partner=partner, queries=queries, step_rows=step_rows, arrivals=arrivals, arrival_routes=arrival_routes, arrival_owners=arrival_owners, new_queries=new_queries, new_step_rows=new_step_rows, value_up=value_up)


def weights_from(first, first_keep, second, second_keep):
    first = jnp.where(first_keep, first, -1e30)
    second = jnp.where(second_keep, second, -1e30)
    peak = jnp.maximum(jnp.max(first, -1, keepdims=True), jnp.max(second, -1, keepdims=True))
    first_w = jnp.where(first_keep, jnp.exp(first - peak), 0.0)
    second_w = jnp.where(second_keep, jnp.exp(second - peak), 0.0)
    total = jnp.sum(first_w, -1, keepdims=True) + jnp.sum(second_w, -1, keepdims=True)
    return first_w.astype(jnp.bfloat16), second_w.astype(jnp.bfloat16), total


def finish(latent_rows, value_up, steps, count, heads):
    latent_rows = latent_rows.reshape(count, steps, heads, LATENT_WIDTH)
    out = jnp.einsum("rshc,hcv->srhv", latent_rows.astype(jnp.float32), value_up.astype(jnp.float32))
    return out.astype(jnp.bfloat16).reshape(steps, count, heads * VD)


def tail_mask(steps, heads):
    query_step = jnp.arange(steps * heads) // heads
    return jnp.arange(steps)[None, None, :] <= query_step[None, :, None]


def resident_block(cache_rows, lens_now, query_rows, step_keys, value_up):
    steps, count, heads = query_rows.shape[0], query_rows.shape[1], query_rows.shape[2]
    score_scale = (VD + KR) ** -0.5
    query_tile = jnp.transpose(query_rows, (1, 0, 2, 3)).reshape(count, steps * heads, KD).astype(jnp.float32)
    trailing_keys = jnp.transpose(step_keys, (1, 0, 2)).astype(jnp.float32)
    primary_keys = cache_rows.astype(jnp.float32)
    primary_part = jnp.einsum("ano,amo->anm", query_tile, primary_keys) * score_scale
    tail_part = jnp.einsum("ano,amo->anm", query_tile, trailing_keys) * score_scale
    keep_main = jnp.arange(cache_rows.shape[1])[None, None, :] < lens_now[:, None, None]
    primary_weights, tail_weights, total = weights_from(primary_part, keep_main, tail_part, tail_mask(steps, heads))
    latent_rows = jnp.einsum("wax,wxe->wae", primary_weights.astype(jnp.float32), primary_keys[..., :LATENT_WIDTH])
    latent_rows = latent_rows + jnp.einsum("wax,wxe->wae", tail_weights.astype(jnp.float32), trailing_keys[..., :LATENT_WIDTH])
    latent_rows = (latent_rows / total).astype(jnp.bfloat16)
    return finish(latent_rows, value_up, steps, count, heads)


def arrival_block(slot_row_index, slot_owner, query_rows, step_keys, value_up):
    steps, count, heads = query_rows.shape[0], query_rows.shape[1], query_rows.shape[2]
    score_scale = (VD + KR) ** -0.5
    query_tile = jnp.transpose(query_rows, (1, 0, 2, 3)).reshape(count, steps * heads, KD).astype(jnp.float32)
    trailing_keys = jnp.transpose(step_keys, (1, 0, 2)).astype(jnp.float32)
    primary_keys = slot_row_index.astype(jnp.float32)
    primary_part = jnp.einsum("uzf,yf->uzy", query_tile, primary_keys) * score_scale
    tail_part = jnp.einsum("ano,amo->anm", query_tile, trailing_keys) * score_scale
    keep_main = slot_owner[None, None, :] == jnp.arange(count, dtype=jnp.int32)[:, None, None]
    primary_weights, tail_weights, total = weights_from(primary_part, keep_main, tail_part, tail_mask(steps, heads))
    latent_rows = jnp.einsum("nmt,tw->nmw", primary_weights.astype(jnp.float32), primary_keys[:, :LATENT_WIDTH])
    latent_rows = latent_rows + jnp.einsum("wax,wxe->wae", tail_weights.astype(jnp.float32), trailing_keys[..., :LATENT_WIDTH])
    latent_rows = (latent_rows / total).astype(jnp.bfloat16)
    return finish(latent_rows, value_up, steps, count, heads)


def reference(latent_cache, cache_lengths, partner, queries, step_rows, arrivals, arrival_routes, arrival_owners, new_queries, new_step_rows, value_up):
    caches = latent_cache.reshape(N_INST, RES_DEV, CTX, KD)
    lengths = cache_lengths.reshape(N_INST, RES_DEV)
    caches = jnp.concatenate([caches[partner, :MIG], caches[:, MIG:]], 1)
    lengths = jnp.concatenate([lengths[partner, :MIG], lengths[:, MIG:]], 1)
    query_inst = jnp.transpose(queries.reshape(STEPS, N_INST, RES_DEV, H, KD), (1, 0, 2, 3, 4))
    step_inst = jnp.transpose(step_rows.reshape(STEPS, N_INST, RES_DEV, KD), (1, 0, 2, 3))
    resident = lax.map(lambda group: resident_block(group[0], group[1], group[2], group[3], value_up), (caches, lengths, query_inst, step_inst))
    resident_out = jnp.transpose(resident, (1, 0, 2, 3)).reshape(STEPS, REQS, H * VD)

    target = arrival_routes[:, 0]
    order = jnp.argsort(target, stable=True)
    sorted_rows = jnp.concatenate([arrivals[order], jnp.zeros((SLOTS, KD), arrivals.dtype)], 0)
    sorted_owner = jnp.concatenate([arrival_owners[order], jnp.full((SLOTS,), -1, jnp.int32)], 0)
    counts = jnp.sum((target[None, :] == jnp.arange(N_INST, dtype=jnp.int32)[:, None]).astype(jnp.int32), 1)
    starts = (jnp.cumsum(counts) - counts).astype(jnp.int32)
    new_inst = jnp.transpose(new_queries.reshape(STEPS, N_INST, NEW_DEV, H, KD), (1, 0, 2, 3, 4))
    new_steps = jnp.transpose(new_step_rows.reshape(STEPS, N_INST, NEW_DEV, KD), (1, 0, 2, 3))

    def one_instance(group):
        start, count, query_rows, step_keys = group
        slot_row_index = lax.dynamic_slice_in_dim(sorted_rows, start, SLOTS, 0)
        slot_owner = lax.dynamic_slice_in_dim(sorted_owner, start, SLOTS, 0)
        slot_owner = jnp.where(jnp.arange(SLOTS, dtype=jnp.int32) < count, slot_owner, -1)
        return arrival_block(slot_row_index, slot_owner, query_rows, step_keys, value_up)

    arrived = lax.map(one_instance, (starts, counts, new_inst, new_steps))
    arrival_out = jnp.transpose(arrived, (1, 0, 2, 3)).reshape(STEPS, NEWS, H * VD)
    return resident_out, arrival_out
```

```python
import jax
import jax.numpy as jnp
from jax import lax
from jax.experimental import pallas as pl
from jax.experimental.pallas import tpu as pltpu
from jax.sharding import PartitionSpec as P

LATENT = 512
KR = 64
VD = 128
KD = 576
KX = 640
LANES = 128
CAP = 16
N_INST = 32
N_HEAD = 8
N_Y = 4
PIECE = 32
PIECES = 18
ROWS_SENT = 80
SENT = ROWS_SENT + PIECE
SCALE = (VD + KR) ** (-0.5)
BIG = 1e30
BF = jnp.bfloat16
F32 = jnp.float32
VMEM_LIMIT = 48 * 1024 * 1024

NT = (((1,), (1,)), ((), ()))


def params(**kw):
    return pltpu.CompilerParams(vmem_limit_bytes=VMEM_LIMIT, **kw)


def vmem():
    return pl.BlockSpec(memory_space=pltpu.VMEM)


def smem():
    return pl.BlockSpec(memory_space=pltpu.SMEM)


def pack_kernel(routes, owners, rows, cache, lens, out):
    n = rows.shape[1]
    route = routes[...]
    hot = (lax.broadcasted_iota(jnp.int32, (N_INST, n), 0) == route).astype(F32)
    upper = (
        lax.broadcasted_iota(jnp.int32, (n, n), 0) <= lax.broadcasted_iota(jnp.int32, (n, n), 1)
    ).astype(BF)
    count = jnp.dot(hot.astype(BF), upper, preferred_element_type=F32)
    rank = jnp.sum(count * hot, 0, keepdims=True) - 1.0
    slot = route * CAP + rank.astype(jnp.int32)
    place = (lax.broadcasted_iota(jnp.int32, (N_INST * CAP, n), 0) == slot).astype(BF)
    owned = (lax.broadcasted_iota(jnp.int32, (KX - KD, n), 0) == owners[...]).astype(BF)
    main = lax.dot_general(place, rows[...], NT, preferred_element_type=F32)
    mark = lax.dot_general(place, owned, NT, preferred_element_type=F32)
    mark = (mark - 1.0) * BIG
    for t in range(4):
        block = main[:, t * LANES : (t + 1) * LANES].astype(BF)
        out[:, t * CAP : (t + 1) * CAP, :] = block.reshape(N_INST, CAP, LANES)
    block = jnp.concatenate([main[:, LATENT:], mark], 1).astype(BF)
    out[:, 4 * CAP : 5 * CAP, :] = block.reshape(N_INST, CAP, LANES)
    for j in range(PIECES):
        out[j, ROWS_SENT:, :] = cache[0, j * PIECE : (j + 1) * PIECE, :]
    for j in range(PIECES, N_INST):
        out[j, ROWS_SENT:, :] = jnp.zeros((PIECE, LANES), BF)
    length = lens[0]
    col = lax.broadcasted_iota(jnp.int32, (PIECE, LANES), 1)
    high = (length // 32).astype(F32)
    low = (length % 32).astype(F32)
    out[PIECES, ROWS_SENT:, :] = jnp.where(col == 0, high, low).astype(BF)


def pack(routes, owners, rows, cache, lens):
    return pl.pallas_call(
        pack_kernel,
        out_shape=jax.ShapeDtypeStruct((N_INST, SENT, LANES), BF),
        in_specs=[vmem(), vmem(), vmem(), pl.BlockSpec((1, KD, LANES), lambda i: (0, 0, 0)), smem()],
        out_specs=pl.BlockSpec((N_INST, SENT, LANES), lambda i: (0, 0, 0)),
        grid=(1,),
        compiler_params=params(),
    )(routes, owners, rows, cache, lens)


def forward_kernel(partner, landed, out, rows):
    for d in range(N_INST):
        out[d] = landed[partner[d], ROWS_SENT:, :]
    rows[...] = landed[:, :ROWS_SENT, :]


def forward(partner, landed):
    return pl.pallas_call(
        forward_kernel,
        out_shape=(
            jax.ShapeDtypeStruct((N_INST, PIECE, LANES), BF),
            jax.ShapeDtypeStruct((N_INST, ROWS_SENT, LANES), BF),
        ),
        in_specs=[smem(), vmem()],
        out_specs=(vmem(), vmem()),
        compiler_params=params(),
    )(partner, landed)


def resident_kernel(info, *refs):
    queries = refs[:N_HEAD]
    keys, tail, out, scores = refs[N_HEAD:]
    me, length = info[0], info[1]
    chunks = keys.shape[0]
    rows = queries[0].shape[0]
    heads = rows // 4
    for b in range(N_HEAD):
        q = queries[b][...]
        for c in range(chunks):
            scores[:, c * LANES : (c + 1) * LANES] = jnp.dot(q, keys[c], preferred_element_type=F32)
        width = chunks * LANES
        last = lax.dot_general(q, tail[...], NT, preferred_element_type=F32)
        tcol = lax.broadcasted_iota(jnp.int32, last.shape, 1)
        step = lax.broadcasted_iota(jnp.int32, last.shape, 0) // heads
        last = jnp.where(tcol <= step, last * SCALE, -BIG)
        col = lax.broadcasted_iota(jnp.int32, (rows, width), 1)
        main = jnp.where(col < length, scores[...] * SCALE, -BIG)
        peak = jnp.maximum(jnp.max(main, -1, keepdims=True), jnp.max(last, -1, keepdims=True))
        main = jnp.exp(main - peak)
        last = jnp.exp(last - peak)
        total = jnp.sum(main, -1, keepdims=True) + jnp.sum(last, -1, keepdims=True)
        acc = jnp.dot(last.astype(BF), tail[:, :LATENT], preferred_element_type=F32)
        main = main.astype(BF)
        for c in range(chunks):
            acc = acc + lax.dot_general(
                main[:, c * LANES : (c + 1) * LANES],
                keys[c, :LATENT, :],
                NT,
                preferred_element_type=F32,
            )
        out[me ^ b] = (acc / total).astype(BF)


def resident(info, queries, keys, tail):
    rows = queries[0].shape[0]
    return pl.pallas_call(
        resident_kernel,
        out_shape=jax.ShapeDtypeStruct((N_HEAD, rows, LATENT), BF),
        in_specs=[smem()] + [vmem()] * (N_HEAD + 2),
        out_specs=vmem(),
        scratch_shapes=[pltpu.VMEM((rows, keys.shape[0] * LANES), F32)],
        compiler_params=params(),
    )(info, *queries, keys, tail)


def arrival_kernel(info, near, far, r0, r1, r2, r3, tail, out_near, stat_near, out_far, keys):
    count = N_INST * CAP
    for i, r in enumerate((r0, r1, r2, r3)):
        for t in range(KX // LANES):
            keys[i * count : (i + 1) * count, t * LANES : (t + 1) * LANES] = r[
                :, t * CAP : (t + 1) * CAP, :
            ].reshape(count, LANES)
    use_tail = info[2]
    rows = near.shape[0]
    tile = 128
    for source in range(2):
        stats = []
        for part in range(rows // tile):
            q = (near, far)[source][part * tile : (part + 1) * tile, :]
            main = lax.dot_general(q, keys[...], NT, preferred_element_type=F32) * SCALE
            last = lax.dot_general(q, tail[...], NT, preferred_element_type=F32) * SCALE
            tstep = lax.broadcasted_iota(jnp.int32, last.shape, 1) // 4
            step = (lax.broadcasted_iota(jnp.int32, last.shape, 0) % 16) // 4
            last = jnp.where(jnp.logical_and(tstep <= step, use_tail > 0), last, -BIG)
            peak = jnp.maximum(jnp.max(main, -1, keepdims=True), jnp.max(last, -1, keepdims=True))
            main = jnp.exp(main - peak)
            last = jnp.exp(last - peak)
            total = jnp.sum(main, -1, keepdims=True) + jnp.sum(last, -1, keepdims=True)
            acc = jnp.dot(main.astype(BF), keys[:, :LATENT], preferred_element_type=F32)
            acc = acc + jnp.dot(last.astype(BF), tail[:, :LATENT], preferred_element_type=F32)
            value = (acc / total).astype(BF)
            lse = peak + jnp.log(total)
            stats.append(jnp.transpose(jnp.broadcast_to(lse, (tile, LANES))))
            if source == 0:
                out_near[part * tile : (part + 1) * tile, :] = value
            else:
                out_far[part * tile : (part + 1) * tile, :] = value
        stat = jnp.concatenate(stats, 1)[:CAP]
        if source == 0:
            stat_near[...] = stat
        else:
            high = stat.astype(BF).astype(F32)
            middle = (stat - high).astype(BF).astype(F32)
            low = stat - high - middle
            row = lax.broadcasted_iota(jnp.int32, stat.shape, 0)
            split = jnp.where(row == 0, high, jnp.where(row == 1, middle, jnp.where(row == 2, low, 0.0)))
            out_far[rows:, :rows] = split.astype(BF)
            out_far[rows:, rows:] = jnp.zeros((CAP, LATENT - rows), BF)


def arrival(info, near, far, rows, tail):
    n = near.shape[0]
    return pl.pallas_call(
        arrival_kernel,
        out_shape=(
            jax.ShapeDtypeStruct((n, LATENT), BF),
            jax.ShapeDtypeStruct((CAP, n), F32),
            jax.ShapeDtypeStruct((n + CAP, LATENT), BF),
        ),
        in_specs=[smem()] + [vmem()] * 7,
        out_specs=(vmem(),) * 3,
        scratch_shapes=[pltpu.VMEM((4 * N_INST * CAP, KX), BF)],
        compiler_params=params(),
    )(info, near, far, *rows, tail)


def combine_kernel(near, stat_near, far, value_up, out):
    n = near.shape[0]
    split = far[n:, :n].astype(F32)
    stat_far = split[0:1] + split[1:2] + split[2:3]
    mine = stat_near[0:1, :]
    top = jnp.maximum(mine, stat_far)
    a, b = jnp.exp(mine - top), jnp.exp(stat_far - top)
    share = a / (a + b)
    share = jnp.transpose(jnp.broadcast_to(share, (LANES, n)))[:, :1]
    value = near[...].astype(F32) * share + far[:n, :].astype(F32) * (1.0 - share)
    value = value.astype(BF)
    for h in range(value_up.shape[0]):
        out[:, h * VD : (h + 1) * VD] = jnp.dot(
            value[h * 16 : (h + 1) * 16], value_up[h], preferred_element_type=F32
        ).astype(BF)


def combine(near, stat_near, far, value_up):
    heads = value_up.shape[0]
    return pl.pallas_call(
        combine_kernel,
        out_shape=jax.ShapeDtypeStruct((16, heads * VD), BF),
        in_specs=[vmem()] * 4,
        out_specs=vmem(),
        compiler_params=params(),
    )(near, stat_near, far, value_up)


def xor_pairs(d):
    return [(h, h ^ d) for h in range(N_HEAD)]


def local(
    latent_cache,
    cache_lengths,
    partner,
    queries,
    step_rows,
    arrivals,
    arrival_routes,
    arrival_owners,
    new_queries,
    new_step_rows,
    value_up,
):
    me = lax.axis_index("head")
    steps, count, heads = queries.shape[0], queries.shape[1], queries.shape[2]
    new_count = new_queries.shape[1]

    cache_t = jnp.transpose(latent_cache, (0, 2, 1))
    sent = pack(
        arrival_routes.reshape(1, -1),
        arrival_owners.reshape(1, -1),
        jnp.transpose(arrivals),
        cache_t,
        cache_lengths,
    )

    hot = jnp.eye(new_count, KX - KD, dtype=BF)
    near = jnp.concatenate(
        [new_queries, jnp.broadcast_to(hot[None, :, None, :], (steps, new_count, heads, KX - KD))], -1
    )
    near = jnp.transpose(near, (2, 0, 1, 3)).reshape(heads * steps * new_count, KX)
    far = lax.ppermute(near, "head", xor_pairs(N_Y))

    q_all = jnp.transpose(queries, (1, 0, 2, 3)).reshape(count, steps * heads, KD)
    q_blocks = []
    for d in range(N_HEAD):
        block = lax.dynamic_index_in_dim(q_all, me ^ d, 0, keepdims=False)
        q_blocks.append(block if d == 0 else lax.ppermute(block, "head", xor_pairs(d)))

    landed = lax.all_to_all(sent, "inst", split_axis=0, concat_axis=0, tiled=True)
    pieces, rows = forward(partner, landed)
    row_blocks = [rows] + [lax.ppermute(rows, "head", xor_pairs(d)) for d in (1, 3, 2)]
    moved = lax.all_to_all(pieces, "inst", split_axis=0, concat_axis=0, tiled=True)
    moved_cache = moved[:PIECES].reshape(1, KD, LANES)
    tag = moved[PIECES, 0, :2].astype(F32)
    moved_len = (tag[0] * 32.0 + tag[1]).astype(jnp.int32)

    full = jnp.concatenate([moved_cache, cache_t[1:]], 0)
    keys = lax.all_to_all(full, "head", split_axis=0, concat_axis=0, tiled=True)
    own_len = lax.dynamic_index_in_dim(cache_lengths, me, 0, keepdims=False)
    length = jnp.where(me == 0, moved_len, own_len)
    info = jnp.stack([me, length, (me < N_Y).astype(jnp.int32)]).astype(jnp.int32)
    tail = lax.dynamic_index_in_dim(step_rows, me, 1, keepdims=False)
    tail = jnp.pad(tail, ((0, LANES - steps), (0, 0)))
    lat = resident(info, q_blocks, keys, tail)
    lat = lax.all_to_all(lat, "head", split_axis=0, concat_axis=0, tiled=True)
    lat = lat.reshape(count, steps, heads, LATENT)
    local_out = jnp.einsum("rshc,hcv->srhv", lat, value_up, preferred_element_type=F32)
    local_out = local_out.astype(BF).reshape(steps, count, heads * VD)

    mark = jnp.where(jnp.arange(KX - KD)[None, :] == jnp.arange(new_count)[:, None], 0.0, -BIG).astype(BF)
    mark = jnp.broadcast_to(mark[None], (steps, new_count, KX - KD))
    new_tail = jnp.concatenate([new_step_rows, mark], -1).reshape(steps * new_count, KX)
    blank = jnp.full((LANES - steps * new_count, KX), 0.0, BF)
    new_tail = jnp.concatenate([new_tail, blank], 0)
    use_tail = jnp.stack([me, length, (me < N_Y).astype(jnp.int32)]).astype(jnp.int32)
    out_near, stat_near, out_far = arrival(use_tail, near, far, row_blocks, new_tail)
    got = lax.ppermute(out_far, "head", xor_pairs(N_Y))
    arrival_out = combine(out_near, stat_near, got, value_up).reshape(steps, new_count, heads * VD)
    return (local_out, arrival_out)


def solution(mesh):
    in_specs = (
        P("inst", "head", None),
        P("inst"),
        P(),
        P(None, "inst", "head", None),
        P(None, "inst", None),
        P(("inst", "head"), None),
        P(("inst", "head"), None),
        P(("inst", "head")),
        P(None, "inst", "head", None),
        P(None, "inst", None),
        P("head", None, None),
    )
    out_specs = (P(None, "inst", "head"), P(None, "inst", "head"))
    return jax.shard_map(local, mesh=mesh, in_specs=in_specs, out_specs=out_specs, check_vma=False)
```

```python
import jax
import jax.numpy as jnp
from jax import lax
from jax.experimental import pallas as pl
from jax.experimental.pallas import tpu as pltpu
from jax.sharding import PartitionSpec as P

LATENT = 512
KR = 64
VD = 128
KD = 576
KX = 640
LANES = 128
CAP = 16
N_INST = 32
N_HEAD = 8
N_Y = 4
PIECE = 24
PIECES = 24
ROWS_SENT = 80
SENT = ROWS_SENT + PIECE
SCALE = (VD + KR) ** (-0.5)
BIG = 1e30
BF = jnp.bfloat16
F32 = jnp.float32
VMEM_LIMIT = 60 * 1024 * 1024

NT = (((1,), (1,)), ((), ()))


def params(limit=32 * 1024 * 1024):
    return pltpu.CompilerParams(vmem_limit_bytes=limit)


def vmem():
    return pl.BlockSpec(memory_space=pltpu.VMEM)


def whole(x):
    return pl.BlockSpec(x.shape, lambda i: (0,) * len(x.shape))


def smem():
    return pl.BlockSpec(memory_space=pltpu.SMEM)


def pack_kernel(lens, routes, owners, rows, cache, out):
    n = rows.shape[1]
    route = routes[...]
    hot = (lax.broadcasted_iota(jnp.int32, (N_INST, n), 0) == route).astype(F32)
    upper = (
        lax.broadcasted_iota(jnp.int32, (n, n), 0) <= lax.broadcasted_iota(jnp.int32, (n, n), 1)
    ).astype(BF)
    count = jnp.dot(hot.astype(BF), upper, preferred_element_type=F32)
    rank = jnp.sum(count * hot, 0, keepdims=True) - 1.0
    slot = route * CAP + rank.astype(jnp.int32)
    place = (lax.broadcasted_iota(jnp.int32, (N_INST * CAP, n), 0) == slot).astype(BF)
    owned = (lax.broadcasted_iota(jnp.int32, (KX - KD, n), 0) == owners[...]).astype(BF)
    main = lax.dot_general(place, rows[...], NT, preferred_element_type=F32)
    mark = lax.dot_general(place, owned, NT, preferred_element_type=F32)
    mark = (mark - 1.0) * BIG
    for t in range(4):
        block = main[:, t * LANES : (t + 1) * LANES].astype(BF)
        out[:, t * CAP : (t + 1) * CAP, :] = block.reshape(N_INST, CAP, LANES)
    block = jnp.concatenate([main[:, LATENT:], mark], 1).astype(BF)
    out[:, 4 * CAP : 5 * CAP, :] = block.reshape(N_INST, CAP, LANES)
    for j in range(PIECES):
        out[j, ROWS_SENT:, :] = cache[0, j * PIECE : (j + 1) * PIECE, :]
    for j in range(PIECES, N_INST):
        out[j, ROWS_SENT:, :] = jnp.zeros((PIECE, LANES), BF)
    length = lens[0]
    col = lax.broadcasted_iota(jnp.int32, (PIECE, LANES), 1)
    high = (length // 32).astype(F32)
    low = (length % 32).astype(F32)
    out[PIECES, ROWS_SENT:, :] = jnp.where(col == 0, high, low).astype(BF)


def pack(routes, owners, rows, cache, lens):
    shape = jax.ShapeDtypeStruct((N_INST, SENT, LANES), BF)
    first = pl.BlockSpec((1, KD, LANES), lambda i: (0, 0, 0))
    return pl.pallas_call(
        pack_kernel,
        out_shape=shape,
        in_specs=[smem(), whole(routes), whole(owners), whole(rows), first],
        out_specs=whole(shape),
        grid=(1,),
        compiler_params=params(VMEM_LIMIT),
    )(lens, routes, owners, rows, cache)


def copy_kernel(x, out):
    out[...] = x[...]


def copied(x):
    block = pl.BlockSpec((1,) + x.shape[1:], lambda i: (i, 0, 0))
    return pl.pallas_call(
        copy_kernel,
        out_shape=jax.ShapeDtypeStruct(x.shape, x.dtype),
        in_specs=[block],
        out_specs=block,
        grid=(x.shape[0],),
        compiler_params=params(),
    )(x)


def settle_kernel(moved, _, out):
    out[0] = moved[...]


def settle(moved, cache):
    return pl.pallas_call(
        settle_kernel,
        out_shape=jax.ShapeDtypeStruct(cache.shape, BF),
        in_specs=[pl.BlockSpec((KD, LANES), lambda i: (0, 0)), pl.BlockSpec(memory_space=pl.ANY)],
        out_specs=pl.BlockSpec((1, KD, LANES), lambda i: (0, 0, 0)),
        grid=(1,),
        input_output_aliases={1: 0},
        compiler_params=params(),
    )(moved, cache)


def forward_kernel(partner, landed, out, rows):
    for d in range(N_INST):
        out[d] = landed[partner[d], ROWS_SENT:, :]
    rows[...] = landed[:, :ROWS_SENT, :]


def forward(partner, landed):
    shapes = (
        jax.ShapeDtypeStruct((N_INST, PIECE, LANES), BF),
        jax.ShapeDtypeStruct((N_INST, ROWS_SENT, LANES), BF),
    )
    return pl.pallas_call(
        forward_kernel,
        out_shape=shapes,
        in_specs=[smem(), vmem()],
        out_specs=(vmem(),) * 2,
        compiler_params=params(),
    )(partner, landed)


def resident_kernel(info, *refs):
    across = refs[:N_Y]
    beyond, chunked, tail, tag, out, query, keys, weights, totals = refs[N_Y:]
    me, length = info[0], info[1]
    side = me // N_Y
    chunks = chunked.shape[0]
    rows = beyond.shape[1]
    heads = rows // 4
    width = chunks * LANES
    for d in range(N_Y):
        query[d * rows : (d + 1) * rows, :] = across[d][side]
        query[(N_Y + d) * rows : (N_Y + d + 1) * rows, :] = beyond[d]
    for c in range(chunks):
        keys[:, c * LANES : (c + 1) * LANES] = chunked[c]
    moved = tag[...].astype(F32)
    moved = (moved[0:1, 0:1] * 32.0 + moved[0:1, 1:2]).astype(jnp.int32)
    length = jnp.where(me == 0, moved, length)
    valid = lax.broadcasted_iota(jnp.int32, (1, width), 1) < length
    tile = 128
    for part in range(N_HEAD * rows // tile):
        span = slice(part * tile, (part + 1) * tile)
        q = query[span, :]
        main = jnp.dot(q, keys[...], preferred_element_type=F32)
        last = lax.dot_general(q, tail[...], NT, preferred_element_type=F32)
        tcol = lax.broadcasted_iota(jnp.int32, last.shape, 1)
        step = lax.broadcasted_iota(jnp.int32, last.shape, 0) % rows // heads
        last = jnp.where(tcol <= step, last * SCALE, -BIG)
        main = jnp.where(valid, main * SCALE, -BIG)
        peak = jnp.maximum(jnp.max(main, -1, keepdims=True), jnp.max(last, -1, keepdims=True))
        main = jnp.exp(main - peak)
        last = jnp.exp(last - peak)
        totals[span, :] = jnp.broadcast_to(
            jnp.sum(main, -1, keepdims=True) + jnp.sum(last, -1, keepdims=True), (tile, LANES)
        )
        weights[span, :width] = main.astype(BF)
        weights[span, width:] = last.astype(BF)
    acc = lax.dot_general(weights[:, :width], keys[:LATENT, :], NT, preferred_element_type=F32)
    acc = acc + jnp.dot(weights[:, width:], tail[:, :LATENT], preferred_element_type=F32)
    for b in range(N_HEAD):
        span = slice(b * rows, (b + 1) * rows)
        out[me ^ b] = (acc[span] / totals[span, :1]).astype(BF)


def resident(info, across, beyond, keys, tail, tag):
    rows = beyond.shape[1]
    count = N_HEAD * rows
    width = keys.shape[0] * LANES
    shape = jax.ShapeDtypeStruct((N_HEAD, rows, LATENT), BF)
    inputs = (*across, beyond, keys, tail, tag)
    return pl.pallas_call(
        resident_kernel,
        out_shape=shape,
        in_specs=[smem()] + [whole(x) for x in inputs],
        out_specs=whole(shape),
        grid=(1,),
        scratch_shapes=[
            pltpu.VMEM((count, KD), BF),
            pltpu.VMEM((KD, width), BF),
            pltpu.VMEM((count, width + LANES), BF),
            pltpu.VMEM((count, LANES), F32),
        ],
        compiler_params=params(VMEM_LIMIT),
    )(info, *inputs)


def arrival_kernel(info, near, far, r0, r1, r2, r3, r4, tail, out_near, stat_near, out_far, keys):
    start = 0
    for r in (r0, r1, r2, r3, r4):
        count = r.shape[0] * CAP
        for t in range(KX // LANES):
            keys[start : start + count, t * LANES : (t + 1) * LANES] = r[
                :, t * CAP : (t + 1) * CAP, :
            ].reshape(count, LANES)
        start = start + count
    use_tail = info[2]
    rows = near.shape[0]
    tile = 256
    for source in range(2):
        stats = []
        for part in range(rows // tile):
            q = (near, far)[source][part * tile : (part + 1) * tile, :]
            main = lax.dot_general(q, keys[...], NT, preferred_element_type=F32) * SCALE
            last = lax.dot_general(q, tail[...], NT, preferred_element_type=F32) * SCALE
            tstep = lax.broadcasted_iota(jnp.int32, last.shape, 1) // 4
            step = (lax.broadcasted_iota(jnp.int32, last.shape, 0) % 16) // 4
            last = jnp.where(jnp.logical_and(tstep <= step, use_tail > 0), last, -BIG)
            peak = jnp.maximum(jnp.max(main, -1, keepdims=True), jnp.max(last, -1, keepdims=True))
            main = jnp.exp(main - peak)
            last = jnp.exp(last - peak)
            total = jnp.sum(main, -1, keepdims=True) + jnp.sum(last, -1, keepdims=True)
            acc = jnp.dot(main.astype(BF), keys[:, :LATENT], preferred_element_type=F32)
            acc = acc + jnp.dot(last.astype(BF), tail[:, :LATENT], preferred_element_type=F32)
            value = (acc / total).astype(BF)
            lse = peak + jnp.log(total)
            stats.append(jnp.transpose(jnp.broadcast_to(lse, (tile, LANES))))
            if source == 0:
                out_near[part * tile : (part + 1) * tile, :] = value
            else:
                out_far[part * tile : (part + 1) * tile, :] = value
        stat = jnp.concatenate(stats, 1)[:CAP]
        if source == 0:
            stat_near[...] = stat
        else:
            high = stat.astype(BF).astype(F32)
            middle = (stat - high).astype(BF).astype(F32)
            low = stat - high - middle
            row = lax.broadcasted_iota(jnp.int32, stat.shape, 0)
            split = jnp.where(row == 0, high, jnp.where(row == 1, middle, jnp.where(row == 2, low, 0.0)))
            out_far[rows:, :rows] = split.astype(BF)
            out_far[rows:, rows:] = jnp.zeros((CAP, LATENT - rows), BF)


def arrival(info, near, far, rows, tail):
    n = near.shape[0]
    shapes = (
        jax.ShapeDtypeStruct((n, LATENT), BF),
        jax.ShapeDtypeStruct((CAP, n), F32),
        jax.ShapeDtypeStruct((n + CAP, LATENT), BF),
    )
    inputs = (near, far, *rows, tail)
    return pl.pallas_call(
        arrival_kernel,
        out_shape=shapes,
        in_specs=[smem()] + [vmem()] * len(inputs),
        out_specs=(vmem(),) * 3,
        scratch_shapes=[pltpu.VMEM((4 * N_INST * CAP, KX), BF)],
        compiler_params=params(),
    )(info, *inputs)


def combine_kernel(near, stat_near, far, value_up, out):
    n = near.shape[0]
    split = far[n:, :n].astype(F32)
    stat_far = split[0:1] + split[1:2] + split[2:3]
    mine = stat_near[0:1, :]
    top = jnp.maximum(mine, stat_far)
    a, b = jnp.exp(mine - top), jnp.exp(stat_far - top)
    share = a / (a + b)
    share = jnp.transpose(jnp.broadcast_to(share, (LANES, n)))[:, :1]
    value = near[...].astype(F32) * share + far[:n, :].astype(F32) * (1.0 - share)
    value = value.astype(BF)
    for h in range(value_up.shape[0]):
        out[:, h * VD : (h + 1) * VD] = jnp.dot(
            value[h * 16 : (h + 1) * 16], value_up[h], preferred_element_type=F32
        ).astype(BF)


def combine(near, stat_near, far, value_up):
    heads = value_up.shape[0]
    return pl.pallas_call(
        combine_kernel,
        out_shape=jax.ShapeDtypeStruct((16, heads * VD), BF),
        in_specs=[vmem()] * 4,
        out_specs=vmem(),
        compiler_params=params(),
    )(near, stat_near, far, value_up)


def xor_pairs(d):
    return [(h, h ^ d) for h in range(N_HEAD)]


def spread(blocks, y, side):
    paired = blocks.reshape((2, N_Y) + blocks.shape[1:])
    across = []
    for d in range(N_Y):
        block = lax.dynamic_index_in_dim(paired, y ^ d, 1, keepdims=False)
        across.append(block if d == 0 else lax.ppermute(block, "head", xor_pairs(d)))
    beyond = jnp.stack([lax.dynamic_index_in_dim(b, 1 - side, 0, keepdims=False) for b in across])
    return across, lax.ppermute(beyond, "head", xor_pairs(N_Y))


def local(
    latent_cache,
    cache_lengths,
    partner,
    queries,
    step_rows,
    arrivals,
    arrival_routes,
    arrival_owners,
    new_queries,
    new_step_rows,
    value_up,
):
    me = lax.axis_index("head")
    steps, count, heads = queries.shape[0], queries.shape[1], queries.shape[2]
    new_count = new_queries.shape[1]

    cache_t = jnp.transpose(latent_cache, (0, 2, 1))
    sent = pack(
        arrival_routes.reshape(1, -1),
        arrival_owners.reshape(1, -1),
        jnp.transpose(arrivals),
        cache_t,
        cache_lengths,
    )

    hot = jnp.eye(new_count, KX - KD, dtype=BF)
    near = jnp.concatenate(
        [new_queries, jnp.broadcast_to(hot[None, :, None, :], (steps, new_count, heads, KX - KD))], -1
    )
    near = jnp.transpose(near, (2, 0, 1, 3)).reshape(heads * steps * new_count, KX)
    y, side = me % N_Y, me // N_Y
    q_all = jnp.transpose(queries, (1, 0, 2, 3)).reshape(count, steps * heads, KD)
    across, beyond = spread(q_all, y, side)

    landed = lax.all_to_all(sent, "inst", split_axis=0, concat_axis=0, tiled=True)
    full = copied(cache_t)
    own_len = lax.dynamic_index_in_dim(cache_lengths, me, 0, keepdims=False)
    info = jnp.stack([me, own_len, (me < N_Y).astype(jnp.int32)]).astype(jnp.int32)
    tail = lax.dynamic_index_in_dim(step_rows, me, 1, keepdims=False)
    tail = jnp.pad(tail, ((0, LANES - steps), (0, 0)))
    mark = jnp.where(jnp.arange(KX - KD)[None, :] == jnp.arange(new_count)[:, None], 0.0, -BIG).astype(BF)
    mark = jnp.broadcast_to(mark[None], (steps, new_count, KX - KD))
    new_tail = jnp.concatenate([new_step_rows, mark], -1).reshape(steps * new_count, KX)
    blank = jnp.full((LANES - steps * new_count, KX), 0.0, BF)
    new_tail = jnp.concatenate([new_tail, blank], 0)
    landed, full, info, tail, new_tail, near, *across = lax.optimization_barrier(
        (landed, full, info, tail, new_tail, near, *across)
    )
    pieces, rows = forward(partner, landed)
    far = lax.ppermute(near, "head", xor_pairs(N_Y))
    half = N_INST // 2
    r1, r3 = (lax.ppermute(rows, "head", xor_pairs(d)) for d in (1, 3))
    moved = lax.all_to_all(pieces, "inst", split_axis=0, concat_axis=0, tiled=True)
    full = settle(moved.reshape(-1, LANES), full)
    r1, r3 = lax.optimization_barrier((r1, r3))
    f1 = lax.ppermute(r3[:half], "head", xor_pairs(1))
    f3 = lax.ppermute(r1[half:], "head", xor_pairs(3))
    full, f1, f3, far, beyond = lax.optimization_barrier((full, f1, f3, far, beyond))
    keys = lax.all_to_all(full, "head", split_axis=0, concat_axis=0, tiled=True)
    row_blocks = (rows, r1, r3, f1, f3)
    out_near, stat_near, out_far = arrival(info, near, far, row_blocks, new_tail)
    got = lax.ppermute(out_far, "head", xor_pairs(N_Y))
    keys, out_far = lax.optimization_barrier((keys, out_far))
    lat = resident(info, across, beyond, keys, tail, moved[PIECES])
    lat = lax.all_to_all(lat, "head", split_axis=0, concat_axis=0, tiled=True)
    lat = lat.reshape(count, steps, heads, LATENT)
    local_out = jnp.einsum("rshc,hcv->srhv", lat, value_up, preferred_element_type=F32)
    local_out = local_out.astype(BF).reshape(steps, count, heads * VD)

    arrival_out = combine(out_near, stat_near, got, value_up).reshape(steps, new_count, heads * VD)
    return (local_out, arrival_out)


def solution(mesh):
    in_specs = (
        P("inst", "head", None),
        P("inst"),
        P(),
        P(None, "inst", "head", None),
        P(None, "inst", None),
        P(("inst", "head"), None),
        P(("inst", "head"), None),
        P(("inst", "head")),
        P(None, "inst", "head", None),
        P(None, "inst", None),
        P("head", None, None),
    )
    out_specs = (P(None, "inst", "head"), P(None, "inst", "head"))
    return jax.shard_map(local, mesh=mesh, in_specs=in_specs, out_specs=out_specs, check_vma=False)
```

```python
import jax
import jax.numpy as jnp
from jax import lax
from jax.experimental import pallas as pl
from jax.experimental.pallas import tpu as pltpu
from jax.sharding import PartitionSpec as P

LATENT = 512
KR = 64
VD = 128
KD = 576
KX = 640
LANES = 128
CAP = 16
N_INST = 32
N_HEAD = 8
N_Y = 4
PIECE = 24
PIECES = 24
ROWS_SENT = 80
SENT = ROWS_SENT + PIECE
SCALE = (VD + KR) ** (-0.5)
BIG = 1e30
BF = jnp.bfloat16
F32 = jnp.float32
VMEM_LIMIT = 60 * 1024 * 1024

NT = (((1,), (1,)), ((), ()))


def params(limit=32 * 1024 * 1024):
    return pltpu.CompilerParams(vmem_limit_bytes=limit)


def vmem():
    return pl.BlockSpec(memory_space=pltpu.VMEM)


def whole(x):
    return pl.BlockSpec(x.shape, lambda i: (0,) * len(x.shape))


def smem():
    return pl.BlockSpec(memory_space=pltpu.SMEM)


def pack_kernel(lens, routes, owners, rows, cache, out):
    n = rows.shape[1]
    route = routes[...]
    hot = (lax.broadcasted_iota(jnp.int32, (N_INST, n), 0) == route).astype(F32)
    upper = (
        lax.broadcasted_iota(jnp.int32, (n, n), 0) <= lax.broadcasted_iota(jnp.int32, (n, n), 1)
    ).astype(BF)
    count = jnp.dot(hot.astype(BF), upper, preferred_element_type=F32)
    rank = jnp.sum(count * hot, 0, keepdims=True) - 1.0
    slot = route * CAP + rank.astype(jnp.int32)
    place = (lax.broadcasted_iota(jnp.int32, (N_INST * CAP, n), 0) == slot).astype(BF)
    owned = (lax.broadcasted_iota(jnp.int32, (KX - KD, n), 0) == owners[...]).astype(BF)
    main = lax.dot_general(place, rows[...], NT, preferred_element_type=F32)
    mark = lax.dot_general(place, owned, NT, preferred_element_type=F32)
    mark = (mark - 1.0) * BIG
    for t in range(4):
        block = main[:, t * LANES : (t + 1) * LANES].astype(BF)
        out[:, t * CAP : (t + 1) * CAP, :] = block.reshape(N_INST, CAP, LANES)
    block = jnp.concatenate([main[:, LATENT:], mark], 1).astype(BF)
    out[:, 4 * CAP : 5 * CAP, :] = block.reshape(N_INST, CAP, LANES)
    for j in range(PIECES):
        out[j, ROWS_SENT:, :] = cache[0, j * PIECE : (j + 1) * PIECE, :]
    for j in range(PIECES, N_INST):
        out[j, ROWS_SENT:, :] = jnp.zeros((PIECE, LANES), BF)
    length = lens[0]
    col = lax.broadcasted_iota(jnp.int32, (PIECE, LANES), 1)
    high = (length // 32).astype(F32)
    low = (length % 32).astype(F32)
    out[PIECES, ROWS_SENT:, :] = jnp.where(col == 0, high, low).astype(BF)


def pack(routes, owners, rows, cache, lens):
    shape = jax.ShapeDtypeStruct((N_INST, SENT, LANES), BF)
    first = pl.BlockSpec((1, KD, LANES), lambda i: (0, 0, 0))
    return pl.pallas_call(
        pack_kernel,
        out_shape=shape,
        in_specs=[smem(), whole(routes), whole(owners), whole(rows), first],
        out_specs=whole(shape),
        grid=(1,),
        compiler_params=params(VMEM_LIMIT),
    )(lens, routes, owners, rows, cache)


def copy_kernel(x, out):
    out[...] = x[...]


def copied(x):
    block = pl.BlockSpec((1,) + x.shape[1:], lambda i: (i, 0, 0))
    return pl.pallas_call(
        copy_kernel,
        out_shape=jax.ShapeDtypeStruct(x.shape, x.dtype),
        in_specs=[block],
        out_specs=block,
        grid=(x.shape[0],),
        compiler_params=params(),
    )(x)


def settle_kernel(moved, _, out):
    out[0] = moved[...]


def settle(moved, cache):
    return pl.pallas_call(
        settle_kernel,
        out_shape=jax.ShapeDtypeStruct(cache.shape, BF),
        in_specs=[pl.BlockSpec((KD, LANES), lambda i: (0, 0)), pl.BlockSpec(memory_space=pl.ANY)],
        out_specs=pl.BlockSpec((1, KD, LANES), lambda i: (0, 0, 0)),
        grid=(1,),
        input_output_aliases={1: 0},
        compiler_params=params(),
    )(moved, cache)


def forward_kernel(partner, landed, out, low, high):
    for d in range(N_INST):
        out[d] = landed[partner[d], ROWS_SENT:, :]
    low[...] = landed[: N_INST // 2, :ROWS_SENT, :]
    high[...] = landed[N_INST // 2 :, :ROWS_SENT, :]


def forward(partner, landed):
    shapes = (
        jax.ShapeDtypeStruct((N_INST, PIECE, LANES), BF),
        jax.ShapeDtypeStruct((N_INST // 2, ROWS_SENT, LANES), BF),
        jax.ShapeDtypeStruct((N_INST // 2, ROWS_SENT, LANES), BF),
    )
    return pl.pallas_call(
        forward_kernel,
        out_shape=shapes,
        in_specs=[smem(), vmem()],
        out_specs=(vmem(),) * 3,
        compiler_params=params(),
    )(partner, landed)


def resident_kernel(info, *refs):
    across = refs[:N_Y]
    beyond, chunked, tail, tag, out, query, keys, weights, totals = refs[N_Y:]
    me, length = info[0], info[1]
    side = me // N_Y
    chunks = chunked.shape[0]
    rows = beyond.shape[1]
    heads = rows // 4
    width = chunks * LANES
    for d in range(N_Y):
        query[d * rows : (d + 1) * rows, :] = across[d][side]
        query[(N_Y + d) * rows : (N_Y + d + 1) * rows, :] = beyond[d]
    for c in range(chunks):
        keys[:, c * LANES : (c + 1) * LANES] = chunked[c]
    moved = tag[...].astype(F32)
    moved = (moved[0:1, 0:1] * 32.0 + moved[0:1, 1:2]).astype(jnp.int32)
    length = jnp.where(me == 0, moved, length)
    valid = lax.broadcasted_iota(jnp.int32, (1, width), 1) < length
    tile = 128
    for part in range(N_HEAD * rows // tile):
        span = slice(part * tile, (part + 1) * tile)
        q = query[span, :]
        main = jnp.dot(q, keys[...], preferred_element_type=F32)
        last = lax.dot_general(q, tail[...], NT, preferred_element_type=F32)
        tcol = lax.broadcasted_iota(jnp.int32, last.shape, 1)
        step = lax.broadcasted_iota(jnp.int32, last.shape, 0) % rows // heads
        last = jnp.where(tcol <= step, last * SCALE, -BIG)
        main = jnp.where(valid, main * SCALE, -BIG)
        peak = jnp.maximum(jnp.max(main, -1, keepdims=True), jnp.max(last, -1, keepdims=True))
        main = jnp.exp(main - peak)
        last = jnp.exp(last - peak)
        totals[span, :] = jnp.broadcast_to(
            jnp.sum(main, -1, keepdims=True) + jnp.sum(last, -1, keepdims=True), (tile, LANES)
        )
        weights[span, :width] = main.astype(BF)
        weights[span, width:] = last.astype(BF)
    acc = lax.dot_general(weights[:, :width], keys[:LATENT, :], NT, preferred_element_type=F32)
    acc = acc + jnp.dot(weights[:, width:], tail[:, :LATENT], preferred_element_type=F32)
    for b in range(N_HEAD):
        span = slice(b * rows, (b + 1) * rows)
        out[me ^ b] = (acc[span] / totals[span, :1]).astype(BF)


def resident(info, across, beyond, keys, tail, tag):
    rows = beyond.shape[1]
    count = N_HEAD * rows
    width = keys.shape[0] * LANES
    shape = jax.ShapeDtypeStruct((N_HEAD, rows, LATENT), BF)
    inputs = (*across, beyond, keys, tail, tag)
    return pl.pallas_call(
        resident_kernel,
        out_shape=shape,
        in_specs=[smem()] + [whole(x) for x in inputs],
        out_specs=whole(shape),
        grid=(1,),
        scratch_shapes=[
            pltpu.VMEM((count, KD), BF),
            pltpu.VMEM((KD, width), BF),
            pltpu.VMEM((count, width + LANES), BF),
            pltpu.VMEM((count, LANES), F32),
        ],
        compiler_params=params(VMEM_LIMIT),
    )(info, *inputs)


def arrival_kernel(info, near, far, tail, *refs):
    row_blocks, (out_near, stat_near, out_far, keys) = refs[:-4], refs[-4:]
    start = 0
    for r in row_blocks:
        count = r.shape[0] * CAP
        for t in range(KX // LANES):
            keys[start : start + count, t * LANES : (t + 1) * LANES] = r[
                :, t * CAP : (t + 1) * CAP, :
            ].reshape(count, LANES)
        start = start + count
    use_tail = info[2]
    rows = near.shape[0]
    tile = 256
    for source in range(2):
        stats = []
        for part in range(rows // tile):
            q = (near, far)[source][part * tile : (part + 1) * tile, :]
            main = lax.dot_general(q, keys[...], NT, preferred_element_type=F32) * SCALE
            last = lax.dot_general(q, tail[...], NT, preferred_element_type=F32) * SCALE
            tstep = lax.broadcasted_iota(jnp.int32, last.shape, 1) // 4
            step = (lax.broadcasted_iota(jnp.int32, last.shape, 0) % 16) // 4
            last = jnp.where(jnp.logical_and(tstep <= step, use_tail > 0), last, -BIG)
            peak = jnp.maximum(jnp.max(main, -1, keepdims=True), jnp.max(last, -1, keepdims=True))
            main = jnp.exp(main - peak)
            last = jnp.exp(last - peak)
            total = jnp.sum(main, -1, keepdims=True) + jnp.sum(last, -1, keepdims=True)
            acc = jnp.dot(main.astype(BF), keys[:, :LATENT], preferred_element_type=F32)
            acc = acc + jnp.dot(last.astype(BF), tail[:, :LATENT], preferred_element_type=F32)
            value = (acc / total).astype(BF)
            lse = peak + jnp.log(total)
            stats.append(jnp.transpose(jnp.broadcast_to(lse, (tile, LANES))))
            if source == 0:
                out_near[part * tile : (part + 1) * tile, :] = value
            else:
                out_far[part * tile : (part + 1) * tile, :] = value
        stat = jnp.concatenate(stats, 1)[:CAP]
        if source == 0:
            stat_near[...] = stat
        else:
            high = stat.astype(BF).astype(F32)
            middle = (stat - high).astype(BF).astype(F32)
            low = stat - high - middle
            row = lax.broadcasted_iota(jnp.int32, stat.shape, 0)
            split = jnp.where(row == 0, high, jnp.where(row == 1, middle, jnp.where(row == 2, low, 0.0)))
            out_far[rows:, :rows] = split.astype(BF)
            out_far[rows:, rows:] = jnp.zeros((CAP, LATENT - rows), BF)


def arrival(info, near, far, rows, tail):
    n = near.shape[0]
    shapes = (
        jax.ShapeDtypeStruct((n, LATENT), BF),
        jax.ShapeDtypeStruct((CAP, n), F32),
        jax.ShapeDtypeStruct((n + CAP, LATENT), BF),
    )
    inputs = (near, far, tail, *rows)
    return pl.pallas_call(
        arrival_kernel,
        out_shape=shapes,
        in_specs=[smem()] + [vmem()] * len(inputs),
        out_specs=(vmem(),) * 3,
        scratch_shapes=[pltpu.VMEM((4 * N_INST * CAP, KX), BF)],
        compiler_params=params(),
    )(info, *inputs)


def combine_kernel(near, stat_near, far, value_up, out):
    n = near.shape[0]
    split = far[n:, :n].astype(F32)
    stat_far = split[0:1] + split[1:2] + split[2:3]
    mine = stat_near[0:1, :]
    top = jnp.maximum(mine, stat_far)
    a, b = jnp.exp(mine - top), jnp.exp(stat_far - top)
    share = a / (a + b)
    share = jnp.transpose(jnp.broadcast_to(share, (LANES, n)))[:, :1]
    value = near[...].astype(F32) * share + far[:n, :].astype(F32) * (1.0 - share)
    value = value.astype(BF)
    for h in range(value_up.shape[0]):
        out[:, h * VD : (h + 1) * VD] = jnp.dot(
            value[h * 16 : (h + 1) * 16], value_up[h], preferred_element_type=F32
        ).astype(BF)


def combine(near, stat_near, far, value_up):
    heads = value_up.shape[0]
    return pl.pallas_call(
        combine_kernel,
        out_shape=jax.ShapeDtypeStruct((16, heads * VD), BF),
        in_specs=[vmem()] * 4,
        out_specs=vmem(),
        compiler_params=params(),
    )(near, stat_near, far, value_up)


def xor_pairs(d):
    return [(h, h ^ d) for h in range(N_HEAD)]


def spread(blocks, y, side):
    paired = blocks.reshape((2, N_Y) + blocks.shape[1:])
    across = []
    for d in range(N_Y):
        block = lax.dynamic_index_in_dim(paired, y ^ d, 1, keepdims=False)
        across.append(block if d == 0 else lax.ppermute(block, "head", xor_pairs(d)))
    return across, jnp.stack([lax.dynamic_index_in_dim(b, 1 - side, 0, keepdims=False) for b in across])


def local(
    latent_cache,
    cache_lengths,
    partner,
    queries,
    step_rows,
    arrivals,
    arrival_routes,
    arrival_owners,
    new_queries,
    new_step_rows,
    value_up,
):
    me = lax.axis_index("head")
    steps, count, heads = queries.shape[0], queries.shape[1], queries.shape[2]
    new_count = new_queries.shape[1]

    cache_t = jnp.transpose(latent_cache, (0, 2, 1))
    sent = pack(
        arrival_routes.reshape(1, -1),
        arrival_owners.reshape(1, -1),
        jnp.transpose(arrivals),
        cache_t,
        cache_lengths,
    )

    hot = jnp.eye(new_count, KX - KD, dtype=BF)
    near = jnp.concatenate(
        [new_queries, jnp.broadcast_to(hot[None, :, None, :], (steps, new_count, heads, KX - KD))], -1
    )
    near = jnp.transpose(near, (2, 0, 1, 3)).reshape(heads * steps * new_count, KX)
    y, side = me % N_Y, me // N_Y
    q_all = jnp.transpose(queries, (1, 0, 2, 3)).reshape(count, steps * heads, KD)
    across, beyond = spread(q_all, y, side)

    landed = lax.all_to_all(sent, "inst", split_axis=0, concat_axis=0, tiled=True)
    full = copied(cache_t)
    own_len = lax.dynamic_index_in_dim(cache_lengths, me, 0, keepdims=False)
    info = jnp.stack([me, own_len, (me < N_Y).astype(jnp.int32)]).astype(jnp.int32)
    tail = lax.dynamic_index_in_dim(step_rows, me, 1, keepdims=False)
    tail = jnp.pad(tail, ((0, LANES - steps), (0, 0)))
    mark = jnp.where(jnp.arange(KX - KD)[None, :] == jnp.arange(new_count)[:, None], 0.0, -BIG).astype(BF)
    mark = jnp.broadcast_to(mark[None], (steps, new_count, KX - KD))
    new_tail = jnp.concatenate([new_step_rows, mark], -1).reshape(steps * new_count, KX)
    blank = jnp.full((LANES - steps * new_count, KX), 0.0, BF)
    new_tail = jnp.concatenate([new_tail, blank], 0)
    landed, full, info, tail, new_tail, near, beyond, *across = lax.optimization_barrier(
        (landed, full, info, tail, new_tail, near, beyond, *across)
    )
    beyond = lax.ppermute(beyond, "head", xor_pairs(N_Y))
    pieces, low, high = forward(partner, landed)
    far = lax.ppermute(near, "head", xor_pairs(N_Y))
    low3 = lax.ppermute(low, "head", xor_pairs(3))
    high1 = lax.ppermute(high, "head", xor_pairs(1))
    moved = lax.all_to_all(pieces, "inst", split_axis=0, concat_axis=0, tiled=True)
    full = settle(moved.reshape(-1, LANES), full)
    f1 = lax.ppermute(low3, "head", xor_pairs(1))
    f3 = lax.ppermute(high1, "head", xor_pairs(3))
    low1 = lax.ppermute(low, "head", xor_pairs(1))
    high3 = lax.ppermute(high, "head", xor_pairs(3))
    full, f1, f3, low1, high3, far, beyond = lax.optimization_barrier((full, f1, f3, low1, high3, far, beyond))
    keys = lax.all_to_all(full, "head", split_axis=0, concat_axis=0, tiled=True)
    row_blocks = (low, high, low1, high1, low3, high3, f1, f3)
    out_near, stat_near, out_far = arrival(info, near, far, row_blocks, new_tail)
    got = lax.ppermute(out_far, "head", xor_pairs(N_Y))
    keys, got = lax.optimization_barrier((keys, got))
    lat = resident(info, across, beyond, keys, tail, moved[PIECES])
    lat = lax.all_to_all(lat, "head", split_axis=0, concat_axis=0, tiled=True)
    lat = lat.reshape(count, steps, heads, LATENT)
    local_out = jnp.einsum("rshc,hcv->srhv", lat, value_up, preferred_element_type=F32)
    local_out = local_out.astype(BF).reshape(steps, count, heads * VD)

    arrival_out = combine(out_near, stat_near, got, value_up).reshape(steps, new_count, heads * VD)
    return (local_out, arrival_out)


def solution(mesh):
    in_specs = (
        P("inst", "head", None),
        P("inst"),
        P(),
        P(None, "inst", "head", None),
        P(None, "inst", None),
        P(("inst", "head"), None),
        P(("inst", "head"), None),
        P(("inst", "head")),
        P(None, "inst", "head", None),
        P(None, "inst", None),
        P("head", None, None),
    )
    out_specs = (P(None, "inst", "head"), P(None, "inst", "head"))
    return jax.shard_map(local, mesh=mesh, in_specs=in_specs, out_specs=out_specs, check_vma=False)
```

```python
import functools

import jax
import jax.numpy as jnp
from jax import lax
from jax.experimental import pallas as pl
from jax.experimental.pallas import tpu as pltpu
from jax.sharding import PartitionSpec as P

LATENT = 512
KR = 64
VD = 128
KD = 576
KX = 640
LANES = 128
CAP = 16
N_INST = 32
N_HEAD = 8
N_Y = 4
PIECE = 24
PIECES = 24
ROWS_SENT = 80
SENT = ROWS_SENT + PIECE
SCALE = (VD + KR) ** (-0.5)
BIG = 1e30
BF = jnp.bfloat16
F32 = jnp.float32
VMEM_LIMIT = 60 * 1024 * 1024

NT = (((1,), (1,)), ((), ()))


def params(limit=32 * 1024 * 1024):
    return pltpu.CompilerParams(vmem_limit_bytes=limit)


def vmem():
    return pl.BlockSpec(memory_space=pltpu.VMEM)


def whole(x):
    return pl.BlockSpec(x.shape, lambda i: (0,) * len(x.shape))


def smem():
    return pl.BlockSpec(memory_space=pltpu.SMEM)


def pack_kernel(lens, routes, owners, rows, cache, out):
    n = rows.shape[1]
    route = routes[...]
    hot = (lax.broadcasted_iota(jnp.int32, (N_INST, n), 0) == route).astype(F32)
    upper = (
        lax.broadcasted_iota(jnp.int32, (n, n), 0) <= lax.broadcasted_iota(jnp.int32, (n, n), 1)
    ).astype(BF)
    count = jnp.dot(hot.astype(BF), upper, preferred_element_type=F32)
    rank = jnp.sum(count * hot, 0, keepdims=True) - 1.0
    slot = route * CAP + rank.astype(jnp.int32)
    place = (lax.broadcasted_iota(jnp.int32, (N_INST * CAP, n), 0) == slot).astype(BF)
    owned = (lax.broadcasted_iota(jnp.int32, (KX - KD, n), 0) == owners[...]).astype(BF)
    main = lax.dot_general(place, rows[...], NT, preferred_element_type=F32)
    mark = lax.dot_general(place, owned, NT, preferred_element_type=F32)
    mark = (mark - 1.0) * BIG
    for t in range(4):
        block = main[:, t * LANES : (t + 1) * LANES].astype(BF)
        out[:, t * CAP : (t + 1) * CAP, :] = block.reshape(N_INST, CAP, LANES)
    block = jnp.concatenate([main[:, LATENT:], mark], 1).astype(BF)
    out[:, 4 * CAP : 5 * CAP, :] = block.reshape(N_INST, CAP, LANES)
    for j in range(PIECES):
        out[j, ROWS_SENT:, :] = cache[0, j * PIECE : (j + 1) * PIECE, :]
    for j in range(PIECES, N_INST):
        out[j, ROWS_SENT:, :] = jnp.zeros((PIECE, LANES), BF)
    length = lens[0]
    col = lax.broadcasted_iota(jnp.int32, (PIECE, LANES), 1)
    high = (length // 32).astype(F32)
    low = (length % 32).astype(F32)
    out[PIECES, ROWS_SENT:, :] = jnp.where(col == 0, high, low).astype(BF)


def pack(routes, owners, rows, cache, lens):
    shape = jax.ShapeDtypeStruct((N_INST, SENT, LANES), BF)
    first = pl.BlockSpec((1, KD, LANES), lambda i: (0, 0, 0))
    return pl.pallas_call(
        pack_kernel,
        out_shape=shape,
        in_specs=[smem(), whole(routes), whole(owners), whole(rows), first],
        out_specs=whole(shape),
        grid=(1,),
        compiler_params=params(VMEM_LIMIT),
    )(lens, routes, owners, rows, cache)


def copy_kernel(x, out):
    out[...] = x[...]


def copied(x):
    block = pl.BlockSpec((1,) + x.shape[1:], lambda i: (i, 0, 0))
    return pl.pallas_call(
        copy_kernel,
        out_shape=jax.ShapeDtypeStruct(x.shape, x.dtype),
        in_specs=[block],
        out_specs=block,
        grid=(x.shape[0],),
        compiler_params=params(),
    )(x)


def settle_kernel(moved, _, out):
    out[0] = moved[...]


def settle(moved, cache):
    return pl.pallas_call(
        settle_kernel,
        out_shape=jax.ShapeDtypeStruct(cache.shape, BF),
        in_specs=[pl.BlockSpec((KD, LANES), lambda i: (0, 0)), pl.BlockSpec(memory_space=pl.ANY)],
        out_specs=pl.BlockSpec((1, KD, LANES), lambda i: (0, 0, 0)),
        grid=(1,),
        input_output_aliases={1: 0},
        compiler_params=params(),
    )(moved, cache)


def forward_kernel(partner, landed, out, low, high):
    for d in range(N_INST):
        out[d] = landed[partner[d], ROWS_SENT:, :]
    low[...] = landed[: N_INST // 2, :ROWS_SENT, :]
    high[...] = landed[N_INST // 2 :, :ROWS_SENT, :]


def forward(partner, landed):
    shapes = (
        jax.ShapeDtypeStruct((N_INST, PIECE, LANES), BF),
        jax.ShapeDtypeStruct((N_INST // 2, ROWS_SENT, LANES), BF),
        jax.ShapeDtypeStruct((N_INST // 2, ROWS_SENT, LANES), BF),
    )
    return pl.pallas_call(
        forward_kernel,
        out_shape=shapes,
        in_specs=[smem(), vmem()],
        out_specs=(vmem(),) * 3,
        compiler_params=params(),
    )(partner, landed)


def resident_kernel(flip, info, *refs):
    n = 1 if flip else N_Y
    blocks, (chunked, tail, tag), rest = refs[:n], refs[n : n + 3], refs[n + 3 :]
    if flip:
        done, rest = rest[0], rest[1:]
    out, query, keys, weights, totals = rest
    me, length = info[0], info[1]
    chunks = chunked.shape[0]
    rows = out.shape[1]
    heads = rows // 4
    width = chunks * LANES
    if flip:
        out[...] = done[...]
    for d in range(N_Y):
        query[d * rows : (d + 1) * rows, :] = blocks[0][d] if flip else blocks[d][me // N_Y]
    for c in range(chunks):
        keys[:, c * LANES : (c + 1) * LANES] = chunked[c]
    moved = tag[...].astype(F32)
    moved = (moved[0:1, 0:1] * 32.0 + moved[0:1, 1:2]).astype(jnp.int32)
    length = jnp.where(me == 0, moved, length)
    valid = lax.broadcasted_iota(jnp.int32, (1, width), 1) < length
    tile = 128
    for part in range(N_Y * rows // tile):
        span = slice(part * tile, (part + 1) * tile)
        q = query[span, :]
        main = jnp.dot(q, keys[...], preferred_element_type=F32)
        last = lax.dot_general(q, tail[...], NT, preferred_element_type=F32)
        tcol = lax.broadcasted_iota(jnp.int32, last.shape, 1)
        step = lax.broadcasted_iota(jnp.int32, last.shape, 0) % rows // heads
        last = jnp.where(tcol <= step, last * SCALE, -BIG)
        main = jnp.where(valid, main * SCALE, -BIG)
        peak = jnp.maximum(jnp.max(main, -1, keepdims=True), jnp.max(last, -1, keepdims=True))
        main = jnp.exp(main - peak)
        last = jnp.exp(last - peak)
        totals[span, :] = jnp.broadcast_to(
            jnp.sum(main, -1, keepdims=True) + jnp.sum(last, -1, keepdims=True), (tile, LANES)
        )
        weights[span, :width] = main.astype(BF)
        weights[span, width:] = last.astype(BF)
    acc = lax.dot_general(weights[:, :width], keys[:LATENT, :], NT, preferred_element_type=F32)
    acc = acc + jnp.dot(weights[:, width:], tail[:, :LATENT], preferred_element_type=F32)
    for d in range(N_Y):
        span = slice(d * rows, (d + 1) * rows)
        out[me ^ (flip * N_Y + d)] = (acc[span] / totals[span, :1]).astype(BF)


def resident(flip, info, blocks, keys, tail, tag, done=()):
    rows = blocks[0].shape[1]
    count = N_Y * rows
    width = keys.shape[0] * LANES
    shape = jax.ShapeDtypeStruct((N_HEAD, rows, LATENT), BF)
    inputs = (*blocks, keys, tail, tag, *done)
    return pl.pallas_call(
        functools.partial(resident_kernel, flip),
        out_shape=shape,
        in_specs=[smem()] + [whole(x) for x in inputs],
        out_specs=whole(shape),
        grid=(1,),
        scratch_shapes=[
            pltpu.VMEM((count, KD), BF),
            pltpu.VMEM((KD, width), BF),
            pltpu.VMEM((count, width + LANES), BF),
            pltpu.VMEM((count, LANES), F32),
        ],
        compiler_params=params(VMEM_LIMIT),
    )(info, *inputs)


def arrival_kernel(send, info, query, tail, *refs):
    if send:
        row_blocks, (out, keys) = refs[:-2], refs[-2:]
    else:
        row_blocks, (out, stat_out, keys) = refs[:-3], refs[-3:]
    start = 0
    for r in row_blocks:
        count = r.shape[0] * CAP
        for t in range(KX // LANES):
            keys[start : start + count, t * LANES : (t + 1) * LANES] = r[
                :, t * CAP : (t + 1) * CAP, :
            ].reshape(count, LANES)
        start = start + count
    use_tail = info[2]
    rows = query.shape[0]
    q = query[...]
    main = lax.dot_general(q, keys[...], NT, preferred_element_type=F32) * SCALE
    last = lax.dot_general(q, tail[...], NT, preferred_element_type=F32) * SCALE
    tstep = lax.broadcasted_iota(jnp.int32, last.shape, 1) // 4
    step = (lax.broadcasted_iota(jnp.int32, last.shape, 0) % 16) // 4
    last = jnp.where(jnp.logical_and(tstep <= step, use_tail > 0), last, -BIG)
    peak = jnp.maximum(jnp.max(main, -1, keepdims=True), jnp.max(last, -1, keepdims=True))
    main = jnp.exp(main - peak)
    last = jnp.exp(last - peak)
    total = jnp.sum(main, -1, keepdims=True) + jnp.sum(last, -1, keepdims=True)
    acc = jnp.dot(main.astype(BF), keys[:, :LATENT], preferred_element_type=F32)
    acc = acc + jnp.dot(last.astype(BF), tail[:, :LATENT], preferred_element_type=F32)
    out[:rows, :] = (acc / total).astype(BF)
    stat = jnp.transpose(jnp.broadcast_to(peak + jnp.log(total), (rows, LANES)))[:CAP]
    if send:
        high = stat.astype(BF).astype(F32)
        middle = (stat - high).astype(BF).astype(F32)
        low = stat - high - middle
        row = lax.broadcasted_iota(jnp.int32, stat.shape, 0)
        split = jnp.where(row == 0, high, jnp.where(row == 1, middle, jnp.where(row == 2, low, 0.0)))
        out[rows:, :rows] = split.astype(BF)
        out[rows:, rows:] = jnp.zeros((CAP, LATENT - rows), BF)
    else:
        stat_out[...] = stat


def arrival(send, info, query, rows, tail):
    n = query.shape[0]
    if send:
        shapes = jax.ShapeDtypeStruct((n + CAP, LATENT), BF)
    else:
        shapes = (jax.ShapeDtypeStruct((n, LATENT), BF), jax.ShapeDtypeStruct((CAP, n), F32))
    inputs = (query, tail, *rows)
    return pl.pallas_call(
        functools.partial(arrival_kernel, send),
        out_shape=shapes,
        in_specs=[smem()] + [vmem()] * len(inputs),
        out_specs=vmem() if send else (vmem(),) * 2,
        scratch_shapes=[pltpu.VMEM((4 * N_INST * CAP, KX), BF)],
        compiler_params=params(),
    )(info, *inputs)


def combine_kernel(near, stat_near, far, value_up, out):
    n = near.shape[0]
    split = far[n:, :n].astype(F32)
    stat_far = split[0:1] + split[1:2] + split[2:3]
    mine = stat_near[0:1, :]
    top = jnp.maximum(mine, stat_far)
    a, b = jnp.exp(mine - top), jnp.exp(stat_far - top)
    share = a / (a + b)
    share = jnp.transpose(jnp.broadcast_to(share, (LANES, n)))[:, :1]
    value = near[...].astype(F32) * share + far[:n, :].astype(F32) * (1.0 - share)
    value = value.astype(BF)
    for h in range(value_up.shape[0]):
        out[:, h * VD : (h + 1) * VD] = jnp.dot(
            value[h * 16 : (h + 1) * 16], value_up[h], preferred_element_type=F32
        ).astype(BF)


def combine(near, stat_near, far, value_up):
    heads = value_up.shape[0]
    return pl.pallas_call(
        combine_kernel,
        out_shape=jax.ShapeDtypeStruct((16, heads * VD), BF),
        in_specs=[vmem()] * 4,
        out_specs=vmem(),
        compiler_params=params(),
    )(near, stat_near, far, value_up)


def xor_pairs(d):
    return [(h, h ^ d) for h in range(N_HEAD)]


def spread(blocks, y, side):
    paired = blocks.reshape((2, N_Y) + blocks.shape[1:])
    across = []
    for d in range(N_Y):
        block = lax.dynamic_index_in_dim(paired, y ^ d, 1, keepdims=False)
        across.append(block if d == 0 else lax.ppermute(block, "head", xor_pairs(d)))
    return across, jnp.stack([lax.dynamic_index_in_dim(b, 1 - side, 0, keepdims=False) for b in across])


def local(
    latent_cache,
    cache_lengths,
    partner,
    queries,
    step_rows,
    arrivals,
    arrival_routes,
    arrival_owners,
    new_queries,
    new_step_rows,
    value_up,
):
    me = lax.axis_index("head")
    steps, count, heads = queries.shape[0], queries.shape[1], queries.shape[2]
    new_count = new_queries.shape[1]

    cache_t = jnp.transpose(latent_cache, (0, 2, 1))
    sent = pack(
        arrival_routes.reshape(1, -1),
        arrival_owners.reshape(1, -1),
        jnp.transpose(arrivals),
        cache_t,
        cache_lengths,
    )

    hot = jnp.eye(new_count, KX - KD, dtype=BF)
    near = jnp.concatenate(
        [new_queries, jnp.broadcast_to(hot[None, :, None, :], (steps, new_count, heads, KX - KD))], -1
    )
    near = jnp.transpose(near, (2, 0, 1, 3)).reshape(heads * steps * new_count, KX)
    y, side = me % N_Y, me // N_Y
    q_all = jnp.transpose(queries, (1, 0, 2, 3)).reshape(count, steps * heads, KD)
    across, beyond = spread(q_all, y, side)

    landed = lax.all_to_all(sent, "inst", split_axis=0, concat_axis=0, tiled=True)
    full = copied(cache_t)
    own_len = lax.dynamic_index_in_dim(cache_lengths, me, 0, keepdims=False)
    info = jnp.stack([me, own_len, (me < N_Y).astype(jnp.int32)]).astype(jnp.int32)
    tail = lax.dynamic_index_in_dim(step_rows, me, 1, keepdims=False)
    tail = jnp.pad(tail, ((0, LANES - steps), (0, 0)))
    mark = jnp.where(jnp.arange(KX - KD)[None, :] == jnp.arange(new_count)[:, None], 0.0, -BIG).astype(BF)
    mark = jnp.broadcast_to(mark[None], (steps, new_count, KX - KD))
    new_tail = jnp.concatenate([new_step_rows, mark], -1).reshape(steps * new_count, KX)
    blank = jnp.full((LANES - steps * new_count, KX), 0.0, BF)
    new_tail = jnp.concatenate([new_tail, blank], 0)
    landed, full, info, tail, new_tail, near, beyond, *across = lax.optimization_barrier(
        (landed, full, info, tail, new_tail, near, beyond, *across)
    )
    beyond = lax.ppermute(beyond, "head", xor_pairs(N_Y))
    pieces, low, high = forward(partner, landed)
    far = lax.ppermute(near, "head", xor_pairs(N_Y))
    low3 = lax.ppermute(low, "head", xor_pairs(3))
    high1 = lax.ppermute(high, "head", xor_pairs(1))
    moved = lax.all_to_all(pieces, "inst", split_axis=0, concat_axis=0, tiled=True)
    full = settle(moved.reshape(-1, LANES), full)
    f1 = lax.ppermute(low3, "head", xor_pairs(1))
    f3 = lax.ppermute(high1, "head", xor_pairs(3))
    low1 = lax.ppermute(low, "head", xor_pairs(1))
    high3 = lax.ppermute(high, "head", xor_pairs(3))
    full, f1, f3, low1, high3, far, beyond = lax.optimization_barrier((full, f1, f3, low1, high3, far, beyond))
    keys = lax.all_to_all(full, "head", split_axis=0, concat_axis=0, tiled=True)
    row_blocks = (low, high, low1, high1, low3, high3, f1, f3)
    out_far = arrival(True, info, far, row_blocks, new_tail)
    got = lax.ppermute(out_far, "head", xor_pairs(N_Y))
    out_near, stat_near = arrival(False, info, near, row_blocks, new_tail)
    keys, out_near = lax.optimization_barrier((keys, out_near))
    first = resident(0, info, across, keys, tail, moved[PIECES])
    first, got = lax.optimization_barrier((first, got))
    lat = resident(1, info, (beyond,), keys, tail, moved[PIECES], (first,))
    lat = lax.all_to_all(lat, "head", split_axis=0, concat_axis=0, tiled=True)
    lat = lat.reshape(count, steps, heads, LATENT)
    local_out = jnp.einsum("rshc,hcv->srhv", lat, value_up, preferred_element_type=F32)
    local_out = local_out.astype(BF).reshape(steps, count, heads * VD)

    arrival_out = combine(out_near, stat_near, got, value_up).reshape(steps, new_count, heads * VD)
    return (local_out, arrival_out)


def solution(mesh):
    in_specs = (
        P("inst", "head", None),
        P("inst"),
        P(),
        P(None, "inst", "head", None),
        P(None, "inst", None),
        P(("inst", "head"), None),
        P(("inst", "head"), None),
        P(("inst", "head")),
        P(None, "inst", "head", None),
        P(None, "inst", None),
        P("head", None, None),
    )
    out_specs = (P(None, "inst", "head"), P(None, "inst", "head"))
    return jax.shard_map(local, mesh=mesh, in_specs=in_specs, out_specs=out_specs, check_vma=False)
```

```python
import functools

import jax
import jax.numpy as jnp
from jax import lax
from jax.experimental import pallas as pl
from jax.experimental.pallas import tpu as pltpu
from jax.sharding import PartitionSpec as P

LATENT = 512
KR = 64
VD = 128
KD = 576
KX = 640
LANES = 128
CAP = 16
N_INST = 32
N_HEAD = 8
N_Y = 4
PIECE = 24
PIECES = 24
ROWS_SENT = 80
SENT = ROWS_SENT + PIECE
SCALE = (VD + KR) ** (-0.5)
BIG = 1e30
BF = jnp.bfloat16
F32 = jnp.float32
VMEM_LIMIT = 60 * 1024 * 1024

NT = (((1,), (1,)), ((), ()))


def params(limit=32 * 1024 * 1024):
    return pltpu.CompilerParams(vmem_limit_bytes=limit)


def vmem():
    return pl.BlockSpec(memory_space=pltpu.VMEM)


def whole(x):
    return pl.BlockSpec(x.shape, lambda i: (0,) * len(x.shape))


def smem():
    return pl.BlockSpec(memory_space=pltpu.SMEM)


def pack_kernel(lens, routes, owners, rows, cache, out):
    n = rows.shape[1]
    route = routes[...]
    hot = (lax.broadcasted_iota(jnp.int32, (N_INST, n), 0) == route).astype(F32)
    upper = (
        lax.broadcasted_iota(jnp.int32, (n, n), 0) <= lax.broadcasted_iota(jnp.int32, (n, n), 1)
    ).astype(BF)
    count = jnp.dot(hot.astype(BF), upper, preferred_element_type=F32)
    rank = jnp.sum(count * hot, 0, keepdims=True) - 1.0
    slot = route * CAP + rank.astype(jnp.int32)
    place = (lax.broadcasted_iota(jnp.int32, (N_INST * CAP, n), 0) == slot).astype(BF)
    owned = (lax.broadcasted_iota(jnp.int32, (KX - KD, n), 0) == owners[...]).astype(BF)
    main = lax.dot_general(place, rows[...], NT, preferred_element_type=F32)
    mark = lax.dot_general(place, owned, NT, preferred_element_type=F32)
    mark = (mark - 1.0) * BIG
    for t in range(4):
        block = main[:, t * LANES : (t + 1) * LANES].astype(BF)
        out[:, t * CAP : (t + 1) * CAP, :] = block.reshape(N_INST, CAP, LANES)
    block = jnp.concatenate([main[:, LATENT:], mark], 1).astype(BF)
    out[:, 4 * CAP : 5 * CAP, :] = block.reshape(N_INST, CAP, LANES)
    for j in range(PIECES):
        out[j, ROWS_SENT:, :] = cache[0, j * PIECE : (j + 1) * PIECE, :]
    for j in range(PIECES, N_INST):
        out[j, ROWS_SENT:, :] = jnp.zeros((PIECE, LANES), BF)
    length = lens[0]
    col = lax.broadcasted_iota(jnp.int32, (PIECE, LANES), 1)
    high = (length // 32).astype(F32)
    low = (length % 32).astype(F32)
    out[PIECES, ROWS_SENT:, :] = jnp.where(col == 0, high, low).astype(BF)


def pack(routes, owners, rows, cache, lens):
    shape = jax.ShapeDtypeStruct((N_INST, SENT, LANES), BF)
    first = pl.BlockSpec((1, KD, LANES), lambda i: (0, 0, 0))
    return pl.pallas_call(
        pack_kernel,
        out_shape=shape,
        in_specs=[smem(), whole(routes), whole(owners), whole(rows), first],
        out_specs=whole(shape),
        grid=(1,),
        compiler_params=params(VMEM_LIMIT),
    )(lens, routes, owners, rows, cache)


def copy_kernel(x, out):
    out[...] = x[...]


def copied(x):
    block = pl.BlockSpec((1,) + x.shape[1:], lambda i: (i, 0, 0))
    return pl.pallas_call(
        copy_kernel,
        out_shape=jax.ShapeDtypeStruct(x.shape, x.dtype),
        in_specs=[block],
        out_specs=block,
        grid=(x.shape[0],),
        compiler_params=params(),
    )(x)


def settle_kernel(moved, _, out):
    out[0] = moved[...]


def settle(moved, cache):
    return pl.pallas_call(
        settle_kernel,
        out_shape=jax.ShapeDtypeStruct(cache.shape, BF),
        in_specs=[pl.BlockSpec((KD, LANES), lambda i: (0, 0)), pl.BlockSpec(memory_space=pl.ANY)],
        out_specs=pl.BlockSpec((1, KD, LANES), lambda i: (0, 0, 0)),
        grid=(1,),
        input_output_aliases={1: 0},
        compiler_params=params(),
    )(moved, cache)


def forward_kernel(partner, landed, out, low, high):
    for d in range(N_INST):
        out[d] = landed[partner[d], ROWS_SENT:, :]
    low[...] = landed[: N_INST // 2, :ROWS_SENT, :]
    high[...] = landed[N_INST // 2 :, :ROWS_SENT, :]


def forward(partner, landed):
    shapes = (
        jax.ShapeDtypeStruct((N_INST, PIECE, LANES), BF),
        jax.ShapeDtypeStruct((N_INST // 2, ROWS_SENT, LANES), BF),
        jax.ShapeDtypeStruct((N_INST // 2, ROWS_SENT, LANES), BF),
    )
    return pl.pallas_call(
        forward_kernel,
        out_shape=shapes,
        in_specs=[smem(), vmem()],
        out_specs=(vmem(),) * 3,
        compiler_params=params(),
    )(partner, landed)


def resident_kernel(flip, info, *refs):
    n = 1 if flip else N_Y
    blocks, (chunked, tail, tag), rest = refs[:n], refs[n : n + 3], refs[n + 3 :]
    if flip:
        done, rest = rest[0], rest[1:]
    out, query, keys, weights, totals = rest
    me, length = info[0], info[1]
    chunks = chunked.shape[0]
    rows = out.shape[1]
    heads = rows // 4
    width = chunks * LANES
    if flip:
        out[...] = done[...]
    for d in range(N_Y):
        query[d * rows : (d + 1) * rows, :] = blocks[0][d] if flip else blocks[d][me // N_Y]
    for c in range(chunks):
        keys[:, c * LANES : (c + 1) * LANES] = chunked[c]
    moved = tag[...].astype(F32)
    moved = (moved[0:1, 0:1] * 32.0 + moved[0:1, 1:2]).astype(jnp.int32)
    length = jnp.where(me == 0, moved, length)
    valid = lax.broadcasted_iota(jnp.int32, (1, width), 1) < length
    tile = 128
    for part in range(N_Y * rows // tile):
        span = slice(part * tile, (part + 1) * tile)
        q = query[span, :]
        main = jnp.dot(q, keys[...], preferred_element_type=F32)
        last = lax.dot_general(q, tail[...], NT, preferred_element_type=F32)
        tcol = lax.broadcasted_iota(jnp.int32, last.shape, 1)
        step = lax.broadcasted_iota(jnp.int32, last.shape, 0) % rows // heads
        last = jnp.where(tcol <= step, last * SCALE, -BIG)
        main = jnp.where(valid, main * SCALE, -BIG)
        peak = jnp.maximum(jnp.max(main, -1, keepdims=True), jnp.max(last, -1, keepdims=True))
        main = jnp.exp(main - peak)
        last = jnp.exp(last - peak)
        totals[span, :] = jnp.broadcast_to(
            jnp.sum(main, -1, keepdims=True) + jnp.sum(last, -1, keepdims=True), (tile, LANES)
        )
        weights[span, :width] = main.astype(BF)
        weights[span, width:] = last.astype(BF)
    acc = lax.dot_general(weights[:, :width], keys[:LATENT, :], NT, preferred_element_type=F32)
    acc = acc + jnp.dot(weights[:, width:], tail[:, :LATENT], preferred_element_type=F32)
    for d in range(N_Y):
        span = slice(d * rows, (d + 1) * rows)
        out[me ^ (flip * N_Y + d)] = (acc[span] / totals[span, :1]).astype(BF)


def resident(flip, info, blocks, keys, tail, tag, done=()):
    rows = blocks[0].shape[1]
    count = N_Y * rows
    width = keys.shape[0] * LANES
    shape = jax.ShapeDtypeStruct((N_HEAD, rows, LATENT), BF)
    inputs = (*blocks, keys, tail, tag, *done)
    return pl.pallas_call(
        functools.partial(resident_kernel, flip),
        out_shape=shape,
        in_specs=[smem()] + [whole(x) for x in inputs],
        out_specs=whole(shape),
        grid=(1,),
        scratch_shapes=[
            pltpu.VMEM((count, KD), BF),
            pltpu.VMEM((KD, width), BF),
            pltpu.VMEM((count, width + LANES), BF),
            pltpu.VMEM((count, LANES), F32),
        ],
        compiler_params=params(VMEM_LIMIT),
    )(info, *inputs)


def arrival_kernel(send, info, query, tail, *refs):
    if send:
        row_blocks, (out, keys) = refs[:-2], refs[-2:]
    else:
        row_blocks, (out, stat_out, keys) = refs[:-3], refs[-3:]
    start = 0
    for r in row_blocks:
        count = r.shape[0] * CAP
        for t in range(KX // LANES):
            keys[start : start + count, t * LANES : (t + 1) * LANES] = r[
                :, t * CAP : (t + 1) * CAP, :
            ].reshape(count, LANES)
        start = start + count
    use_tail = info[2]
    rows = query.shape[0]
    tile = 128
    stats = []
    for part in range(rows // tile):
        span = slice(part * tile, (part + 1) * tile)
        q = query[span, :]
        main = lax.dot_general(q, keys[...], NT, preferred_element_type=F32) * SCALE
        last = lax.dot_general(q, tail[...], NT, preferred_element_type=F32) * SCALE
        tstep = lax.broadcasted_iota(jnp.int32, last.shape, 1) // 4
        step = (lax.broadcasted_iota(jnp.int32, last.shape, 0) % 16) // 4
        last = jnp.where(jnp.logical_and(tstep <= step, use_tail > 0), last, -BIG)
        peak = jnp.maximum(jnp.max(main, -1, keepdims=True), jnp.max(last, -1, keepdims=True))
        main = jnp.exp(main - peak)
        last = jnp.exp(last - peak)
        total = jnp.sum(main, -1, keepdims=True) + jnp.sum(last, -1, keepdims=True)
        acc = jnp.dot(main.astype(BF), keys[:, :LATENT], preferred_element_type=F32)
        acc = acc + jnp.dot(last.astype(BF), tail[:, :LATENT], preferred_element_type=F32)
        out[span, :] = (acc / total).astype(BF)
        stats.append(jnp.transpose(jnp.broadcast_to(peak + jnp.log(total), (tile, LANES)))[:CAP])
    stat = jnp.concatenate(stats, 1)
    if send:
        high = stat.astype(BF).astype(F32)
        middle = (stat - high).astype(BF).astype(F32)
        low = stat - high - middle
        row = lax.broadcasted_iota(jnp.int32, stat.shape, 0)
        split = jnp.where(row == 0, high, jnp.where(row == 1, middle, jnp.where(row == 2, low, 0.0)))
        out[rows:, :rows] = split.astype(BF)
        out[rows:, rows:] = jnp.zeros((CAP, LATENT - rows), BF)
    else:
        stat_out[...] = stat


def arrival(send, info, query, rows, tail):
    n = query.shape[0]
    if send:
        shapes = jax.ShapeDtypeStruct((n + CAP, LATENT), BF)
    else:
        shapes = (jax.ShapeDtypeStruct((n, LATENT), BF), jax.ShapeDtypeStruct((CAP, n), F32))
    inputs = (query, tail, *rows)
    return pl.pallas_call(
        functools.partial(arrival_kernel, send),
        out_shape=shapes,
        in_specs=[smem()] + [vmem()] * len(inputs),
        out_specs=vmem() if send else (vmem(),) * 2,
        scratch_shapes=[pltpu.VMEM((4 * N_INST * CAP, KX), BF)],
        compiler_params=params(),
    )(info, *inputs)


def combine_kernel(near, stat_near, far, value_up, out):
    n = near.shape[0]
    split = far[n:, :n].astype(F32)
    stat_far = split[0:1] + split[1:2] + split[2:3]
    mine = stat_near[0:1, :]
    top = jnp.maximum(mine, stat_far)
    a, b = jnp.exp(mine - top), jnp.exp(stat_far - top)
    share = a / (a + b)
    share = jnp.transpose(jnp.broadcast_to(share, (LANES, n)))[:, :1]
    value = near[...].astype(F32) * share + far[:n, :].astype(F32) * (1.0 - share)
    value = value.astype(BF)
    for h in range(value_up.shape[0]):
        out[:, h * VD : (h + 1) * VD] = jnp.dot(
            value[h * 16 : (h + 1) * 16], value_up[h], preferred_element_type=F32
        ).astype(BF)


def combine(near, stat_near, far, value_up):
    heads = value_up.shape[0]
    return pl.pallas_call(
        combine_kernel,
        out_shape=jax.ShapeDtypeStruct((16, heads * VD), BF),
        in_specs=[vmem()] * 4,
        out_specs=vmem(),
        compiler_params=params(),
    )(near, stat_near, far, value_up)


def xor_pairs(d):
    return [(h, h ^ d) for h in range(N_HEAD)]


def spread(blocks, y, side):
    paired = blocks.reshape((2, N_Y) + blocks.shape[1:])
    across = []
    for d in range(N_Y):
        block = lax.dynamic_index_in_dim(paired, y ^ d, 1, keepdims=False)
        across.append(block if d == 0 else lax.ppermute(block, "head", xor_pairs(d)))
    return across, jnp.stack([lax.dynamic_index_in_dim(b, 1 - side, 0, keepdims=False) for b in across])


def local(
    latent_cache,
    cache_lengths,
    partner,
    queries,
    step_rows,
    arrivals,
    arrival_routes,
    arrival_owners,
    new_queries,
    new_step_rows,
    value_up,
):
    me = lax.axis_index("head")
    steps, count, heads = queries.shape[0], queries.shape[1], queries.shape[2]
    new_count = new_queries.shape[1]

    cache_t = jnp.transpose(latent_cache, (0, 2, 1))
    sent = pack(
        arrival_routes.reshape(1, -1),
        arrival_owners.reshape(1, -1),
        jnp.transpose(arrivals),
        cache_t,
        cache_lengths,
    )

    hot = jnp.eye(new_count, KX - KD, dtype=BF)
    near = jnp.concatenate(
        [new_queries, jnp.broadcast_to(hot[None, :, None, :], (steps, new_count, heads, KX - KD))], -1
    )
    near = jnp.transpose(near, (2, 0, 1, 3)).reshape(heads * steps * new_count, KX)
    y, side = me % N_Y, me // N_Y
    q_all = jnp.transpose(queries, (1, 0, 2, 3)).reshape(count, steps * heads, KD)
    across, beyond = spread(q_all, y, side)

    landed = lax.all_to_all(sent, "inst", split_axis=0, concat_axis=0, tiled=True)
    full = copied(cache_t)
    own_len = lax.dynamic_index_in_dim(cache_lengths, me, 0, keepdims=False)
    info = jnp.stack([me, own_len, (me < N_Y).astype(jnp.int32)]).astype(jnp.int32)
    tail = lax.dynamic_index_in_dim(step_rows, me, 1, keepdims=False)
    tail = jnp.pad(tail, ((0, LANES - steps), (0, 0)))
    mark = jnp.where(jnp.arange(KX - KD)[None, :] == jnp.arange(new_count)[:, None], 0.0, -BIG).astype(BF)
    mark = jnp.broadcast_to(mark[None], (steps, new_count, KX - KD))
    new_tail = jnp.concatenate([new_step_rows, mark], -1).reshape(steps * new_count, KX)
    blank = jnp.full((LANES - steps * new_count, KX), 0.0, BF)
    new_tail = jnp.concatenate([new_tail, blank], 0)
    landed, full, info, tail, new_tail, near, beyond, *across = lax.optimization_barrier(
        (landed, full, info, tail, new_tail, near, beyond, *across)
    )
    beyond = lax.ppermute(beyond, "head", xor_pairs(N_Y))
    pieces, low, high = forward(partner, landed)
    far = lax.ppermute(near, "head", xor_pairs(N_Y))
    low3 = lax.ppermute(low, "head", xor_pairs(3))
    high1 = lax.ppermute(high, "head", xor_pairs(1))
    moved = lax.all_to_all(pieces, "inst", split_axis=0, concat_axis=0, tiled=True)
    full = settle(moved.reshape(-1, LANES), full)
    f1 = lax.ppermute(low3, "head", xor_pairs(1))
    f3 = lax.ppermute(high1, "head", xor_pairs(3))
    low1 = lax.ppermute(low, "head", xor_pairs(1))
    high3 = lax.ppermute(high, "head", xor_pairs(3))
    full, f1, f3, low1, high3, far, beyond = lax.optimization_barrier((full, f1, f3, low1, high3, far, beyond))
    keys = lax.all_to_all(full, "head", split_axis=0, concat_axis=0, tiled=True)
    row_blocks = (low, high, low1, high1, low3, high3, f1, f3)
    out_far = arrival(True, info, far, row_blocks, new_tail)
    got = lax.ppermute(out_far, "head", xor_pairs(N_Y))
    out_near, stat_near = arrival(False, info, near, row_blocks, new_tail)
    keys, out_near = lax.optimization_barrier((keys, out_near))
    first = resident(0, info, across, keys, tail, moved[PIECES])
    first, got = lax.optimization_barrier((first, got))
    lat = resident(1, info, (beyond,), keys, tail, moved[PIECES], (first,))
    lat = lax.all_to_all(lat, "head", split_axis=0, concat_axis=0, tiled=True)
    lat = lat.reshape(count, steps, heads, LATENT)
    local_out = jnp.einsum("rshc,hcv->srhv", lat, value_up, preferred_element_type=F32)
    local_out = local_out.astype(BF).reshape(steps, count, heads * VD)

    arrival_out = combine(out_near, stat_near, got, value_up).reshape(steps, new_count, heads * VD)
    return (local_out, arrival_out)


def solution(mesh):
    in_specs = (
        P("inst", "head", None),
        P("inst"),
        P(),
        P(None, "inst", "head", None),
        P(None, "inst", None),
        P(("inst", "head"), None),
        P(("inst", "head"), None),
        P(("inst", "head")),
        P(None, "inst", "head", None),
        P(None, "inst", None),
        P("head", None, None),
    )
    out_specs = (P(None, "inst", "head"), P(None, "inst", "head"))
    return jax.shard_map(local, mesh=mesh, in_specs=in_specs, out_specs=out_specs, check_vma=False)
```
